32 devices in a mesh: dp: 4 (over y, core), expert: 8 (over z, x).
Axes of the slice: x: 2, y: 2, z: 4, core: 2. Of those that a mesh axis runs over, the one named last changes fastest.
Arguments:
- tokens: bfloat16 [4096, 1024], P(('dp', 'expert')), may hold values from -6 to 6
- cotangent: bfloat16 [4096, 1024], P(('dp', 'expert')), may hold values from -6 to 6
- picks: int32 [32, 16], P(('dp', 'expert')), may hold values from 0 to 127
- gates: float32 [32, 16], P(('dp', 'expert')), may hold values from 0.1 to 1
- w_gate: bfloat16 [16, 2816, 1024], P('expert', 'dp'), may hold values from -0.1875 to 0.1875
- w_up: bfloat16 [16, 2816, 1024], P('expert', 'dp'), may hold values from -0.1875 to 0.1875
- w_down: bfloat16 [16, 2816, 1024], P('expert', 'dp'), may hold values from -0.109375 to 0.109375
Outputs:
- grad_tokens: bfloat16 [4096, 1024], P(('dp', 'expert'))
- grad_gate: bfloat16 [16, 2816, 1024], P('expert', 'dp')
- grad_up: bfloat16 [16, 2816, 1024], P('expert', 'dp')
- grad_down: bfloat16 [16, 2816, 1024], P('expert', 'dp')
The draws below stay inside these ranges and needn't reach their ends.
Inputs may be any that keep to these rules, and one draw needn't show every extreme that they name: picks[s, e] is the row, among the 128 tokens of device s, that expert e takes from device s.
All inputs are finite; a program needn't handle non-finite values.
Results may differ from the reference program's by a relative error of at most 0.02.
Values may be sent and summed in bfloat16 or wider, within the bound.
A program may use at most 64 MiB of HBM per device.

```python
import math
import jax
import jax.numpy as jnp
from jax import lax

D = 1024
F = 2816
TOK_DEV = 128
E = 16
SOURCES = 32
TOKENS = 4096
N_DP = 4


def place_ends(values, rng, least, largest):
    spot = [jax.random.randint(jax.random.fold_in(rng, axis), (), 0, length) for axis, length in enumerate(values.shape)]
    widest = values.shape.index(max(values.shape))
    beside = spot[:widest] + [(spot[widest] + 1) % values.shape[widest]] + spot[widest + 1:]
    return values.at[tuple(spot)].set(least).at[tuple(beside)].set(largest)


def block_scale(key, shape, cuts, low, high):
    level, own = 1.0, jax.random.fold_in(key, 6)
    for axis_at, blocks in cuts:
        heights = jnp.exp(jax.random.uniform(jax.random.fold_in(own, axis_at), (blocks,), jnp.float32, low / len(cuts), high / len(cuts)))
        level = level * jnp.repeat(heights, shape[axis_at] // blocks).reshape([-1 if axis == axis_at else 1 for axis in range(len(shape))])
    return level


def normal_values(stream_key, extent, spread, bound, shards=(), kind=jnp.bfloat16):
    entries = spread * jax.random.normal(stream_key, extent, jnp.float32)
    if shards:
        entries = entries * block_scale(stream_key, extent, shards, -0.22, 0.18)
    return jnp.clip(entries, -bound, bound).astype(kind)


def setup_inputs(seed: int = 0) -> dict:
    key_list = jax.random.split(jax.random.key(seed), 8)
    return {
        "tokens": normal_values(key_list[0], (TOKENS, D), 1.0, 6.0, ((0, 32),)),
        "cotangent": normal_values(key_list[1], (TOKENS, D), 1.0, 6.0, ((0, 32),)),
        "picks": place_ends(jax.random.randint(key_list[2], (SOURCES, E), 0, TOK_DEV), jax.random.fold_in(key_list[2], 1), 0, TOK_DEV - 1).astype(jnp.int32),
        "gates": jnp.clip(jnp.exp(math.log(1.0) - 2.3025851 * jax.random.uniform(key_list[3], (SOURCES, E), jnp.float32) ** block_scale(key_list[3], (SOURCES, E), ((0, 32),), -0.2, 0.2)), 0.1, 1.0),
        "w_gate": normal_values(key_list[4], (E, F, D), D ** -0.5, 0.1875, ((0, 8), (1, 4))),
        "w_up": normal_values(key_list[5], (E, F, D), D ** -0.5, 0.1875, ((0, 8), (1, 4))),
        "w_down": normal_values(key_list[6], (E, F, D), F ** -0.5, 0.109375, ((0, 8), (1, 4))),
    }


def reference(tokens, cotangent, picks, gates, w_gate, w_up, w_down):
    base = (jnp.arange(SOURCES, dtype=jnp.int32) * TOK_DEV)[:, None]
    indices = (picks + base).astype(jnp.int32).T
    weights_t = gates.T
    block = F // N_DP

    def expert(args):
        rows_idx, gate_col, wg, wu, wd = args
        inputs = tokens[rows_idx]
        scaled = (cotangent[rows_idx].astype(jnp.float32) * gate_col[:, None]).astype(jnp.bfloat16)
        pre_gate = jnp.dot(inputs, wg.T, preferred_element_type=jnp.float32)
        pre_up = jnp.dot(inputs, wu.T, preferred_element_type=jnp.float32)
        sigmoid_g = jax.nn.sigmoid(pre_gate)
        active = pre_gate * sigmoid_g
        hidden = (active * pre_up).astype(jnp.bfloat16)
        grad_hidden = jnp.dot(scaled, wd.T, preferred_element_type=jnp.float32)
        g_down = jnp.dot(hidden.T, scaled, preferred_element_type=jnp.float32).astype(jnp.bfloat16)
        d_up = (grad_hidden * active).astype(jnp.bfloat16)
        d_gate = (grad_hidden * pre_up * sigmoid_g * (1.0 + pre_gate * (1.0 - sigmoid_g))).astype(jnp.bfloat16)
        g_gate = jnp.dot(d_gate.T, inputs, preferred_element_type=jnp.float32).astype(jnp.bfloat16)
        g_up = jnp.dot(d_up.T, inputs, preferred_element_type=jnp.float32).astype(jnp.bfloat16)
        dg_blocks = d_gate.astype(jnp.float32).reshape(SOURCES, N_DP, block)
        du_blocks = d_up.astype(jnp.float32).reshape(SOURCES, N_DP, block)
        wg_blocks = wg.astype(jnp.float32).reshape(N_DP, block, D)
        wu_blocks = wu.astype(jnp.float32).reshape(N_DP, block, D)
        parts = jnp.einsum("snf,nfd->snd", dg_blocks, wg_blocks) + jnp.einsum("snf,nfd->snd", du_blocks, wu_blocks)
        rows = jnp.sum(parts.astype(jnp.bfloat16).astype(jnp.float32), axis=1)
        return g_gate, g_up, g_down, rows

    grad_gate, grad_up, grad_down, all_rows = lax.map(expert, (indices, weights_t, w_gate, w_up, w_down))
    flat_idx = indices.reshape(-1)
    total = jnp.zeros((TOKENS, D), jnp.float32).at[flat_idx].add(all_rows.reshape(-1, D))
    return total.astype(jnp.bfloat16), grad_gate, grad_up, grad_down
```

```python
import functools

import jax
import jax.numpy as jnp
from jax import lax
from jax.experimental import pallas as pl
from jax.experimental.pallas import tpu as pltpu
from jax.sharding import PartitionSpec as P

LANES = 128
BF16 = jnp.bfloat16
F32 = jnp.float32
NT = (((1,), (1,)), ((), ()))


def bulk_wait(ref, count, sem):
    part = ref.at[pl.ds(0, count)]
    pltpu.make_async_copy(part, part, sem).wait()


def exchange_kernel(
    n_dp,
    n_ex,
    picks_ref,
    gates_ref,
    tokens_hbm,
    cot_hbm,
    wg_hbm,
    wu_hbm,
    wd_hbm,
    x_out,
    dy_out,
    dt_out,
    back_out,
    tok,
    cot,
    wg,
    wu,
    wd,
    wide,
    xmsg,
    dymsg,
    xbuf,
    dybuf,
    partmsg,
    backbuf,
    load_sem,
    send_sem,
    recv_sem,
):
    n = n_dp * n_ex
    experts, _, width = wg.shape
    chunks = width // LANES
    picked = picks_ref.shape[1]
    token_rows = tok.shape[0]
    rows = n * experts
    my_dp, my_ex = lax.axis_index("dp"), lax.axis_index("expert")
    me = my_dp * n_ex + my_ex

    loads = [
        pltpu.make_async_copy(src, dst, load_sem.at[i])
        for i, (src, dst) in enumerate(
            ((tokens_hbm, tok), (cot_hbm, cot), (wg_hbm, wg), (wu_hbm, wu), (wd_hbm, wd))
        )
    ]
    for load in loads:
        load.start()

    def peer(step):
        other = lax.rem(me + step, n)
        return other, (other // n_ex, lax.rem(other, n_ex))

    barrier = pltpu.get_barrier_semaphore()

    def greet(step, carry):
        _, where = peer(step)
        pl.semaphore_signal(
            barrier, inc=1, device_id=where, device_id_type=pl.DeviceIdType.MESH
        )
        return carry

    lax.fori_loop(1, n, greet, 0)

    eye = lax.broadcasted_iota(jnp.int32, (picked, picked), 0) == lax.broadcasted_iota(
        jnp.int32, (picked, picked), 1
    )
    pick_col = jnp.sum(
        jnp.where(eye, picks_ref[...].astype(F32), 0.0), axis=1, keepdims=True
    ).astype(jnp.int32)
    gate_col = jnp.sum(jnp.where(eye, gates_ref[...], 0.0), axis=1, keepdims=True)
    selector = jnp.where(
        lax.broadcasted_iota(jnp.int32, (picked, token_rows), 1) == pick_col, 1.0, 0.0
    ).astype(BF16)

    def pack(value, msg):
        count = value.shape[0]
        for k in range(chunks):
            wide[pl.ds(k, count, stride=chunks), :] = value[:, k * LANES : (k + 1) * LANES]
        msg[...] = wide[pl.ds(0, count * chunks), :].astype(BF16).reshape(msg.shape)

    def unpack(buf, out):
        wide[...] = buf[...].reshape(wide.shape).astype(F32)
        for k in range(chunks):
            out[:, k * LANES : (k + 1) * LANES] = wide[pl.ds(k, rows, stride=chunks), :].astype(
                BF16
            )

    def send_all(msg, buf, slot, by_expert):
        def one(step, carry):
            other, where = peer(step)
            pltpu.make_async_remote_copy(
                src_ref=msg.at[where[1] if by_expert else other],
                dst_ref=buf.at[me],
                send_sem=send_sem.at[slot],
                recv_sem=recv_sem.at[slot],
                device_id=where,
                device_id_type=pl.DeviceIdType.MESH,
            ).start()
            return carry

        lax.fori_loop(1, n, one, 0)
        buf[me] = msg[my_ex if by_expert else me]

    loads[0].wait()
    pack(jnp.dot(selector, tok[...], preferred_element_type=F32), xmsg)
    pl.semaphore_wait(barrier, n - 1)
    send_all(xmsg, xbuf, 0, True)
    loads[1].wait()
    pack(jnp.dot(selector, cot[...], preferred_element_type=F32) * gate_col, dymsg)
    send_all(dymsg, dybuf, 1, True)

    expert_of = lax.rem(lax.broadcasted_iota(jnp.int32, (rows, 1), 0), experts)

    def forward(value, weights):
        total = lax.dot_general(value, weights[0], NT, preferred_element_type=F32)
        for e in range(1, experts):
            total = jnp.where(
                expert_of == e,
                lax.dot_general(value, weights[e], NT, preferred_element_type=F32),
                total,
            )
        return total

    bulk_wait(xbuf, n - 1, recv_sem.at[0])
    unpack(xbuf, x_out)
    x = x_out[...]
    loads[2].wait()
    pre_gate = forward(x, wg)
    loads[3].wait()
    pre_up = forward(x, wu)
    sigmoid_g = jax.nn.sigmoid(pre_gate)
    active = pre_gate * sigmoid_g
    hidden = active * pre_up
    slope = pre_up * sigmoid_g * (1.0 + pre_gate * (1.0 - sigmoid_g))
    loads[4].wait()
    bulk_wait(dybuf, n - 1, recv_sem.at[1])
    unpack(dybuf, dy_out)
    grad_hidden = forward(dy_out[...], wd)
    d_up = grad_hidden * active
    d_gate = grad_hidden * slope

    part = jnp.zeros((rows, width), F32)
    for e in range(experts):
        mine = expert_of == e
        part += jnp.dot(
            jnp.where(mine, d_gate, 0.0).astype(BF16), wg[e], preferred_element_type=F32
        )
        part += jnp.dot(
            jnp.where(mine, d_up, 0.0).astype(BF16), wu[e], preferred_element_type=F32
        )
    pack(part, partmsg)
    send_all(partmsg, backbuf, 2, False)
    dt_out[0] = d_gate.T.astype(BF16)
    dt_out[1] = d_up.T.astype(BF16)
    dt_out[2] = hidden.T.astype(BF16)
    bulk_wait(backbuf, n - 1, recv_sem.at[2])
    unpack(backbuf, back_out)
    bulk_wait(xbuf, n - 1, send_sem.at[0])
    bulk_wait(dybuf, n - 1, send_sem.at[1])
    bulk_wait(partmsg, n - 1, send_sem.at[2])


def grads_kernel(
    n_dp, experts, picks_ref, back_ref, x_ref, dy_ref, dt_ref, tokens_out, gate_out, up_out, down_out
):
    expert = pl.program_id(0)

    @pl.when((expert == 0) & (pl.program_id(1) == 0))
    def _():
        shape = (tokens_out.shape[0], picks_ref.shape[1])
        chosen = jnp.where(
            lax.broadcasted_iota(jnp.int32, shape, 0) == picks_ref[...], 1.0, 0.0
        )
        spread = jnp.concatenate([chosen] * n_dp, axis=1).astype(BF16)
        tokens_out[...] = jnp.dot(
            spread, back_ref[...], preferred_element_type=F32
        ).astype(BF16)

    rows = x_ref.shape[0]
    lane = lax.broadcasted_iota(jnp.int32, (1, rows), 1)
    mine = jnp.where(lax.rem(lane, experts) == expert, 1.0, 0.0).astype(BF16)
    for i, (out, other) in enumerate(((gate_out, x_ref), (up_out, x_ref), (down_out, dy_ref))):
        out[0] = jnp.dot(dt_ref[i] * mine, other[...], preferred_element_type=F32).astype(BF16)


def shards(n_dp, n_ex, tokens, cotangent, picks, gates, w_gate, w_up, w_down):
    token_rows, width = tokens.shape
    experts, hidden, _ = w_gate.shape
    n = n_dp * n_ex
    rows = n * experts
    message = (experts * width // LANES, LANES)
    weight = pltpu.VMEM((experts, hidden, width), BF16)
    vmem = pl.BlockSpec(memory_space=pltpu.VMEM)
    anywhere = pl.BlockSpec(memory_space=pl.ANY)
    x, dy, dt, back = pl.pallas_call(
        functools.partial(exchange_kernel, n_dp, n_ex),
        out_shape=(
            jax.ShapeDtypeStruct((rows, width), BF16),
            jax.ShapeDtypeStruct((rows, width), BF16),
            jax.ShapeDtypeStruct((3, hidden, rows), BF16),
            jax.ShapeDtypeStruct((rows, width), BF16),
        ),
        in_specs=[vmem] * 2 + [anywhere] * 5,
        out_specs=(vmem,) * 4,
        scratch_shapes=[
            pltpu.VMEM((token_rows, width), BF16),
            pltpu.VMEM((token_rows, width), BF16),
            weight,
            weight,
            weight,
            pltpu.VMEM((rows * width // LANES, LANES), F32),
            pltpu.VMEM((n_ex,) + message, BF16),
            pltpu.VMEM((n_ex,) + message, BF16),
            pltpu.VMEM((n,) + message, BF16),
            pltpu.VMEM((n,) + message, BF16),
            pltpu.VMEM((n,) + message, BF16),
            pltpu.VMEM((n,) + message, BF16),
            pltpu.SemaphoreType.DMA((5,)),
            pltpu.SemaphoreType.DMA((3,)),
            pltpu.SemaphoreType.DMA((3,)),
        ],
        compiler_params=pltpu.CompilerParams(
            collective_id=0, has_side_effects=True, vmem_limit_bytes=56 * 1024 * 1024
        ),
    )(picks, gates, tokens, cotangent, w_gate, w_up, w_down)

    step = max(d for d in range(16, 177, 16) if hidden % d == 0)
    whole = lambda *shape: pl.BlockSpec(shape, lambda e, f: (0,) * len(shape))
    tile = pl.BlockSpec((1, step, width), lambda e, f: (e, f, 0))
    grad = jax.ShapeDtypeStruct(w_gate.shape, BF16)
    return pl.pallas_call(
        functools.partial(grads_kernel, n_dp, experts),
        grid=(experts, hidden // step),
        out_shape=(jax.ShapeDtypeStruct(tokens.shape, BF16), grad, grad, grad),
        in_specs=[
            whole(*picks.shape),
            whole(rows, width),
            whole(rows, width),
            whole(rows, width),
            pl.BlockSpec((3, step, rows), lambda e, f: (0, f, 0)),
        ],
        out_specs=(whole(*tokens.shape), tile, tile, tile),
        compiler_params=pltpu.CompilerParams(vmem_limit_bytes=48 * 1024 * 1024),
    )(picks, back, x, dy, dt)


def solution(mesh):
    spread = P(("dp", "expert"), None)
    weight = P("expert", "dp", None)
    return jax.shard_map(
        functools.partial(shards, mesh.shape["dp"], mesh.shape["expert"]),
        mesh=mesh,
        in_specs=(spread,) * 4 + (weight,) * 3,
        out_specs=(spread,) + (weight,) * 3,
        check_vma=False,
    )
```

```python
import functools

import jax
import jax.numpy as jnp
from jax import lax
from jax.experimental import pallas as pl
from jax.experimental.pallas import tpu as pltpu
from jax.sharding import PartitionSpec as P

LANES = 128
BF16 = jnp.bfloat16
F32 = jnp.float32
NT = (((1,), (1,)), ((), ()))


def block_of(hidden_units):
    return max(d for d in range(16, 177, 16) if hidden_units % d == 0)


def bulk_wait(ref, count, sem):
    part = ref.at[pl.ds(0, count)]
    pltpu.make_async_copy(part, part, sem).wait()


def exchange_kernel(
    n_dp,
    n_ex,
    picks_ref,
    gates_ref,
    tokens_hbm,
    cot_hbm,
    wg_hbm,
    wu_hbm,
    wd_hbm,
    back_out,
    gate_out,
    up_out,
    down_out,
    x_out,
    dy_out,
    dt_out,
    tok,
    cot,
    wg,
    wu,
    wd,
    wide,
    xmsg,
    dymsg,
    xbuf,
    dybuf,
    partmsg,
    backbuf,
    load_sem,
    send_sem,
    recv_sem,
):
    n = n_dp * n_ex
    experts, _, width = wg.shape
    chunks = width // LANES
    picked = picks_ref.shape[1]
    token_rows = tok.shape[0]
    rows = n * experts
    my_dp, my_ex = lax.axis_index("dp"), lax.axis_index("expert")
    me = my_dp * n_ex + my_ex

    loads = [
        pltpu.make_async_copy(src, dst, load_sem.at[i])
        for i, (src, dst) in enumerate(
            ((tokens_hbm, tok), (cot_hbm, cot), (wg_hbm, wg), (wu_hbm, wu), (wd_hbm, wd))
        )
    ]
    for load in loads:
        load.start()

    def peer(step):
        other = lax.rem(me + step, n)
        return other, (other // n_ex, lax.rem(other, n_ex))

    barrier = pltpu.get_barrier_semaphore()

    def greet(step, carry):
        _, where = peer(step)
        pl.semaphore_signal(
            barrier, inc=1, device_id=where, device_id_type=pl.DeviceIdType.MESH
        )
        return carry

    lax.fori_loop(1, n, greet, 0)

    eye = lax.broadcasted_iota(jnp.int32, (picked, picked), 0) == lax.broadcasted_iota(
        jnp.int32, (picked, picked), 1
    )
    pick_col = jnp.sum(
        jnp.where(eye, picks_ref[...].astype(F32), 0.0), axis=1, keepdims=True
    ).astype(jnp.int32)
    gate_col = jnp.sum(jnp.where(eye, gates_ref[...], 0.0), axis=1, keepdims=True)
    selector = jnp.where(
        lax.broadcasted_iota(jnp.int32, (picked, token_rows), 1) == pick_col, 1.0, 0.0
    ).astype(BF16)

    def pack(value, msg):
        count = value.shape[0]
        for k in range(chunks):
            wide[pl.ds(k, count, stride=chunks), :] = value[:, k * LANES : (k + 1) * LANES]
        msg[...] = wide[pl.ds(0, count * chunks), :].astype(BF16).reshape(msg.shape)

    def unpack(buf, out):
        wide[...] = buf[...].reshape(wide.shape).astype(F32)
        for k in range(chunks):
            out[:, k * LANES : (k + 1) * LANES] = wide[pl.ds(k, rows, stride=chunks), :].astype(
                BF16
            )

    def send_all(msg, buf, slot, by_expert):
        def one(step, carry):
            other, where = peer(step)
            pltpu.make_async_remote_copy(
                src_ref=msg.at[where[1] if by_expert else other],
                dst_ref=buf.at[me],
                send_sem=send_sem.at[slot],
                recv_sem=recv_sem.at[slot],
                device_id=where,
                device_id_type=pl.DeviceIdType.MESH,
            ).start()
            return carry

        lax.fori_loop(1, n, one, 0)
        buf[me] = msg[my_ex if by_expert else me]

    loads[0].wait()
    pack(jnp.dot(selector, tok[...], preferred_element_type=F32), xmsg)
    pl.semaphore_wait(barrier, n - 1)
    send_all(xmsg, xbuf, 0, True)
    loads[1].wait()
    pack(jnp.dot(selector, cot[...], preferred_element_type=F32) * gate_col, dymsg)
    send_all(dymsg, dybuf, 1, True)

    expert_of = lax.rem(lax.broadcasted_iota(jnp.int32, (rows, 1), 0), experts)

    def forward(value, weights):
        total = lax.dot_general(value, weights[0], NT, preferred_element_type=F32)
        for e in range(1, experts):
            total = jnp.where(
                expert_of == e,
                lax.dot_general(value, weights[e], NT, preferred_element_type=F32),
                total,
            )
        return total

    bulk_wait(xbuf, n - 1, recv_sem.at[0])
    unpack(xbuf, x_out)
    x = x_out[...]
    loads[2].wait()
    pre_gate = forward(x, wg)
    loads[3].wait()
    pre_up = forward(x, wu)
    sigmoid_g = jax.nn.sigmoid(pre_gate)
    active = pre_gate * sigmoid_g
    hidden = active * pre_up
    slope = pre_up * sigmoid_g * (1.0 + pre_gate * (1.0 - sigmoid_g))
    loads[4].wait()
    bulk_wait(dybuf, n - 1, recv_sem.at[1])
    unpack(dybuf, dy_out)
    grad_hidden = forward(dy_out[...], wd)
    d_up = grad_hidden * active
    d_gate = grad_hidden * slope

    part = jnp.zeros((rows, width), F32)
    for e in range(experts):
        mine = expert_of == e
        part += jnp.dot(
            jnp.where(mine, d_gate, 0.0).astype(BF16), wg[e], preferred_element_type=F32
        )
        part += jnp.dot(
            jnp.where(mine, d_up, 0.0).astype(BF16), wu[e], preferred_element_type=F32
        )
    pack(part, partmsg)
    send_all(partmsg, backbuf, 2, False)
    dt_out[0] = d_gate.T.astype(BF16)
    dt_out[1] = d_up.T.astype(BF16)
    dt_out[2] = hidden.T.astype(BF16)
    lane_expert = lax.rem(lax.broadcasted_iota(jnp.int32, (1, rows), 1), experts)
    hidden_units = wg.shape[1]
    block = block_of(hidden_units)
    for e in range(experts):
        mine = jnp.where(lane_expert == e, 1.0, 0.0).astype(BF16)

        def grads(i, carry):
            at = pl.ds(pl.multiple_of(i * block, block), block)
            for j, (out, other) in enumerate(
                ((gate_out, x_out), (up_out, x_out), (down_out, dy_out))
            ):
                out[e, at, :] = jnp.dot(
                    dt_out[j, at, :] * mine, other[...], preferred_element_type=F32
                ).astype(BF16)
            return carry

        lax.fori_loop(0, hidden_units // block, grads, 0)
    bulk_wait(backbuf, n - 1, recv_sem.at[2])
    unpack(backbuf, back_out)
    bulk_wait(xbuf, n - 1, send_sem.at[0])
    bulk_wait(dybuf, n - 1, send_sem.at[1])
    bulk_wait(partmsg, n - 1, send_sem.at[2])


def store_kernel(
    n_dp,
    picks_ref,
    back_hbm,
    gate_in,
    up_in,
    down_in,
    tokens_out,
    gate_out,
    up_out,
    down_out,
    back,
    total,
    sem,
):
    load = pltpu.make_async_copy(back_hbm, back, sem.at[0])
    load.start()
    stores = [
        pltpu.make_async_copy(src, dst, sem.at[1 + i])
        for i, (src, dst) in enumerate(
            ((gate_in, gate_out), (up_in, up_out), (down_in, down_out))
        )
    ]
    for store in stores:
        store.start()
    shape = (total.shape[0], picks_ref.shape[1])
    chosen = jnp.where(lax.broadcasted_iota(jnp.int32, shape, 0) == picks_ref[...], 1.0, 0.0)
    spread = jnp.concatenate([chosen] * n_dp, axis=1).astype(BF16)
    load.wait()
    total[...] = jnp.dot(spread, back[...], preferred_element_type=F32).astype(BF16)
    stores.append(pltpu.make_async_copy(total, tokens_out, sem.at[4]))
    stores[-1].start()
    for store in stores:
        store.wait()


def shards(n_dp, n_ex, tokens, cotangent, picks, gates, w_gate, w_up, w_down):
    picks, gates, tokens, cotangent, w_gate, w_up, w_down = (
        pltpu.with_memory_space_constraint(a, pltpu.HBM)
        for a in (picks, gates, tokens, cotangent, w_gate, w_up, w_down)
    )
    token_rows, width = tokens.shape
    experts, hidden, _ = w_gate.shape
    n = n_dp * n_ex
    rows = n * experts
    message = (experts * width // LANES, LANES)
    weight = pltpu.VMEM((experts, hidden, width), BF16)
    vmem = pl.BlockSpec(memory_space=pltpu.VMEM)
    anywhere = pl.BlockSpec(memory_space=pl.ANY)
    back, d_gate, d_up, d_down = pl.pallas_call(
        functools.partial(exchange_kernel, n_dp, n_ex),
        out_shape=(pltpu.VMEM((rows, width), BF16),) + (weight,) * 3,
        in_specs=[vmem] * 2 + [anywhere] * 5,
        out_specs=(vmem,) * 4,
        scratch_shapes=[
            pltpu.VMEM((rows, width), BF16),
            pltpu.VMEM((rows, width), BF16),
            pltpu.VMEM((3, hidden, rows), BF16),
            pltpu.VMEM((token_rows, width), BF16),
            pltpu.VMEM((token_rows, width), BF16),
            weight,
            weight,
            weight,
            pltpu.VMEM((rows * width // LANES, LANES), F32),
            pltpu.VMEM((n_ex,) + message, BF16),
            pltpu.VMEM((n_ex,) + message, BF16),
            pltpu.VMEM((n,) + message, BF16),
            pltpu.VMEM((n,) + message, BF16),
            pltpu.VMEM((n,) + message, BF16),
            pltpu.VMEM((n,) + message, BF16),
            pltpu.SemaphoreType.DMA((5,)),
            pltpu.SemaphoreType.DMA((3,)),
            pltpu.SemaphoreType.DMA((3,)),
        ],
        compiler_params=pltpu.CompilerParams(
            collective_id=0, has_side_effects=True, vmem_limit_bytes=28 * 1024 * 1024
        ),
    )(picks, gates, tokens, cotangent, w_gate, w_up, w_down)

    grad = jax.ShapeDtypeStruct(w_gate.shape, BF16)
    return pl.pallas_call(
        functools.partial(store_kernel, n_dp),
        out_shape=(jax.ShapeDtypeStruct(tokens.shape, BF16), grad, grad, grad),
        in_specs=[vmem] + [anywhere] * 4,
        out_specs=(anywhere,) * 4,
        scratch_shapes=[
            pltpu.VMEM((rows, width), BF16),
            pltpu.VMEM(tokens.shape, BF16),
            pltpu.SemaphoreType.DMA((5,)),
        ],
        compiler_params=pltpu.CompilerParams(vmem_limit_bytes=8 * 1024 * 1024),
    )(picks, back, d_gate, d_up, d_down)


def solution(mesh):
    spread = P(("dp", "expert"), None)
    weight = P("expert", "dp", None)
    return jax.shard_map(
        functools.partial(shards, mesh.shape["dp"], mesh.shape["expert"]),
        mesh=mesh,
        in_specs=(spread,) * 4 + (weight,) * 3,
        out_specs=(spread,) + (weight,) * 3,
        check_vma=False,
    )
```

```python
import functools

import jax
import jax.numpy as jnp
from jax import lax
from jax.experimental import pallas as pl
from jax.experimental.pallas import tpu as pltpu
from jax.sharding import PartitionSpec as P

LANES = 128
BF16 = jnp.bfloat16
F32 = jnp.float32
NT = (((1,), (1,)), ((), ()))


def block_of(hidden_units):
    return max(d for d in range(16, 177, 16) if hidden_units % d == 0)


def bulk_wait(ref, count, sem):
    part = ref.at[pl.ds(0, count)]
    pltpu.make_async_copy(part, part, sem).wait()


def exchange_kernel(
    n_dp,
    n_ex,
    picks_ref,
    gates_ref,
    tokens_hbm,
    cot_hbm,
    wg_hbm,
    wu_hbm,
    wd_hbm,
    back_out,
    gate_out,
    up_out,
    down_out,
    x_out,
    dy_out,
    dt_out,
    tok,
    cot,
    wg,
    wu,
    wd,
    wide,
    xmsg,
    dymsg,
    xbuf,
    dybuf,
    partmsg,
    backbuf,
    load_sem,
    send_sem,
    recv_sem,
):
    n = n_dp * n_ex
    experts, _, width = wg.shape
    chunks = width // LANES
    picked = picks_ref.shape[1]
    token_rows = tok.shape[0]
    my_dp, my_ex = lax.axis_index("dp"), lax.axis_index("expert")
    me = my_dp * n_ex + my_ex

    loads = [
        pltpu.make_async_copy(src, dst, load_sem.at[i])
        for i, (src, dst) in enumerate(
            ((tokens_hbm, tok), (cot_hbm, cot), (wg_hbm, wg), (wu_hbm, wu), (wd_hbm, wd))
        )
    ]
    for load in loads:
        load.start()

    def wrap(value, size):
        return jnp.where(value >= size, value - size, value)

    experts_at = [wrap(my_ex + b, n_ex) for b in range(n_ex)]

    def each_peer(act):
        for b in range(1, n_ex):
            act(my_dp, experts_at[b])

        def ring(a, carry):
            at_dp = wrap(my_dp + a, n_dp)
            for b in range(n_ex):
                act(at_dp, experts_at[b])
            return carry

        lax.fori_loop(1, n_dp, ring, 0)

    barrier = pltpu.get_barrier_semaphore()

    def greet(dp, ex):
        pl.semaphore_signal(
            barrier, inc=1, device_id=(dp, ex), device_id_type=pl.DeviceIdType.MESH
        )

    each_peer(greet)

    eye = lax.broadcasted_iota(jnp.int32, (picked, picked), 0) == lax.broadcasted_iota(
        jnp.int32, (picked, picked), 1
    )
    pick_col = jnp.sum(
        jnp.where(eye, picks_ref[...].astype(F32), 0.0), axis=1, keepdims=True
    ).astype(jnp.int32)
    gate_col = jnp.sum(jnp.where(eye, gates_ref[...], 0.0), axis=1, keepdims=True)
    selector = jnp.where(
        lax.broadcasted_iota(jnp.int32, (picked, token_rows), 1) == pick_col, 1.0, 0.0
    ).astype(BF16)

    def pack(parts, msg):
        count = parts[0].shape[0]
        stride = len(parts) * chunks
        for e, value in enumerate(parts):
            for k in range(chunks):
                wide[pl.ds(e * chunks + k, count, stride=stride), :] = value[
                    :, k * LANES : (k + 1) * LANES
                ]
        msg[...] = wide[pl.ds(0, count * stride), :].astype(BF16).reshape(msg.shape)

    def unpack(buf, out):
        wide[...] = buf[...].reshape(wide.shape).astype(F32)
        for e in range(experts):
            for k in range(chunks):
                out[e, :, k * LANES : (k + 1) * LANES] = wide[
                    pl.ds(e * chunks + k, n, stride=experts * chunks), :
                ].astype(BF16)

    def send_all(msg, buf, slot, by_expert):
        def one(dp, ex):
            pltpu.make_async_remote_copy(
                src_ref=msg.at[ex if by_expert else dp * n_ex + ex],
                dst_ref=buf.at[me],
                send_sem=send_sem.at[slot],
                recv_sem=recv_sem.at[slot],
                device_id=(dp, ex),
                device_id_type=pl.DeviceIdType.MESH,
            ).start()

        each_peer(one)
        buf[me] = msg[my_ex if by_expert else me]

    loads[0].wait()
    pack([jnp.dot(selector, tok[...], preferred_element_type=F32)], xmsg)
    pl.semaphore_wait(barrier, n - 1)
    send_all(xmsg, xbuf, 0, True)
    loads[1].wait()
    pack([jnp.dot(selector, cot[...], preferred_element_type=F32) * gate_col], dymsg)
    send_all(dymsg, dybuf, 1, True)

    def forward(e, value, weights):
        return lax.dot_general(value[e], weights[e], NT, preferred_element_type=F32)

    every = range(experts)
    bulk_wait(xbuf, n - 1, recv_sem.at[0])
    unpack(xbuf, x_out)
    loads[2].wait()
    pre_gate = [forward(e, x_out, wg) for e in every]
    loads[3].wait()
    pre_up = [forward(e, x_out, wu) for e in every]
    sigmoid_g = [jax.nn.sigmoid(g) for g in pre_gate]
    active = [g * s for g, s in zip(pre_gate, sigmoid_g)]
    slope = [
        u * s * (1.0 + g * (1.0 - s)) for g, u, s in zip(pre_gate, pre_up, sigmoid_g)
    ]
    for e in every:
        dt_out[e, 2] = (active[e] * pre_up[e]).T.astype(BF16)
    loads[4].wait()
    bulk_wait(dybuf, n - 1, recv_sem.at[1])
    unpack(dybuf, dy_out)
    grad_hidden = [forward(e, dy_out, wd) for e in every]
    d_up = [h * a for h, a in zip(grad_hidden, active)]
    d_gate = [h * s for h, s in zip(grad_hidden, slope)]
    pack(
        [
            jnp.dot(d_gate[e].astype(BF16), wg[e], preferred_element_type=F32)
            + jnp.dot(d_up[e].astype(BF16), wu[e], preferred_element_type=F32)
            for e in every
        ],
        partmsg,
    )
    send_all(partmsg, backbuf, 2, False)
    hidden_units = wg.shape[1]
    block = block_of(hidden_units)
    for e in every:
        dt_out[e, 0] = d_gate[e].T.astype(BF16)
        dt_out[e, 1] = d_up[e].T.astype(BF16)

        def grads(i, carry):
            at = pl.ds(pl.multiple_of(i * block, block), block)
            for j, (out, other) in enumerate(
                ((gate_out, x_out), (up_out, x_out), (down_out, dy_out))
            ):
                out[e, at, :] = jnp.dot(
                    dt_out[e, j, at, :], other[e], preferred_element_type=F32
                ).astype(BF16)
            return carry

        lax.fori_loop(0, hidden_units // block, grads, 0)
    bulk_wait(backbuf, n - 1, recv_sem.at[2])
    unpack(backbuf, back_out)
    bulk_wait(xbuf, n - 1, send_sem.at[0])
    bulk_wait(dybuf, n - 1, send_sem.at[1])
    bulk_wait(partmsg, n - 1, send_sem.at[2])


def store_kernel(
    n_dp,
    n_ex,
    picks_ref,
    back_hbm,
    gate_in,
    up_in,
    down_in,
    tokens_out,
    gate_out,
    up_out,
    down_out,
    back,
    total,
    sem,
    store_sem,
):
    load = pltpu.make_async_copy(back_hbm, back, sem.at[0])
    load.start()
    experts, hidden_units, _ = gate_in.shape
    half = hidden_units // 2 // 16 * 16
    stores = []
    for e in range(experts):
        for src, dst in ((gate_in, gate_out), (up_in, up_out), (down_in, down_out)):
            for at in (pl.ds(0, half), pl.ds(half, hidden_units - half)):
                stores.append(
                    pltpu.make_async_copy(
                        src.at[e, at], dst.at[e, at], store_sem.at[len(stores)]
                    )
                )
                stores[-1].start()
    token_rows = total.shape[0]
    picks = picks_ref[...].astype(F32)
    load.wait()
    columns = lax.broadcasted_iota(jnp.int32, (picks.shape[1], n_dp * n_ex), 0)
    places = lax.broadcasted_iota(jnp.int32, (picks.shape[1], n_dp * n_ex), 1)
    summed = jnp.zeros(total.shape, F32)
    for e in range(experts):
        wanted = jnp.where(columns == lax.rem(places, n_ex) * experts + e, 1.0, 0.0)
        row = jnp.dot(
            jnp.broadcast_to(picks, (8, picks.shape[1])).astype(BF16),
            wanted.astype(BF16),
            preferred_element_type=F32,
        )[:1]
        chosen = jnp.where(
            lax.broadcasted_iota(jnp.int32, (token_rows, n_dp * n_ex), 0).astype(F32) == row,
            1.0,
            0.0,
        ).astype(BF16)
        summed += jnp.dot(chosen, back[e], preferred_element_type=F32)
    total[...] = summed.astype(BF16)
    stores.append(pltpu.make_async_copy(total, tokens_out, sem.at[1]))
    stores[-1].start()
    for store in stores:
        store.wait()


def shards(n_dp, n_ex, tokens, cotangent, picks, gates, w_gate, w_up, w_down):
    picks, gates, tokens, cotangent, w_gate, w_up, w_down = (
        pltpu.with_memory_space_constraint(a, pltpu.HBM)
        for a in (picks, gates, tokens, cotangent, w_gate, w_up, w_down)
    )
    token_rows, width = tokens.shape
    experts, hidden, _ = w_gate.shape
    n = n_dp * n_ex
    rows = (experts, n, width)
    message = (experts * width // LANES, LANES)
    weight = pltpu.VMEM((experts, hidden, width), BF16)
    vmem = pl.BlockSpec(memory_space=pltpu.VMEM)
    anywhere = pl.BlockSpec(memory_space=pl.ANY)
    back, d_gate, d_up, d_down = pl.pallas_call(
        functools.partial(exchange_kernel, n_dp, n_ex),
        out_shape=(pltpu.VMEM(rows, BF16),) + (weight,) * 3,
        in_specs=[vmem] * 2 + [anywhere] * 5,
        out_specs=(vmem,) * 4,
        scratch_shapes=[
            pltpu.VMEM(rows, BF16),
            pltpu.VMEM(rows, BF16),
            pltpu.VMEM((experts, 3, hidden, n), BF16),
            pltpu.VMEM((token_rows, width), BF16),
            pltpu.VMEM((token_rows, width), BF16),
            weight,
            weight,
            weight,
            pltpu.VMEM((n * experts * width // LANES, LANES), F32),
            pltpu.VMEM((n_ex,) + message, BF16),
            pltpu.VMEM((n_ex,) + message, BF16),
            pltpu.VMEM((n,) + message, BF16),
            pltpu.VMEM((n,) + message, BF16),
            pltpu.VMEM((n,) + message, BF16),
            pltpu.VMEM((n,) + message, BF16),
            pltpu.SemaphoreType.DMA((5,)),
            pltpu.SemaphoreType.DMA((3,)),
            pltpu.SemaphoreType.DMA((3,)),
        ],
        compiler_params=pltpu.CompilerParams(
            collective_id=0, has_side_effects=True, vmem_limit_bytes=28 * 1024 * 1024
        ),
    )(picks, gates, tokens, cotangent, w_gate, w_up, w_down)

    grad = jax.ShapeDtypeStruct(w_gate.shape, BF16)
    return pl.pallas_call(
        functools.partial(store_kernel, n_dp, n_ex),
        out_shape=(jax.ShapeDtypeStruct(tokens.shape, BF16), grad, grad, grad),
        in_specs=[vmem] + [anywhere] * 4,
        out_specs=(anywhere,) * 4,
        scratch_shapes=[
            pltpu.VMEM(rows, BF16),
            pltpu.VMEM(tokens.shape, BF16),
            pltpu.SemaphoreType.DMA((2,)),
            pltpu.SemaphoreType.DMA((6 * experts,)),
        ],
        compiler_params=pltpu.CompilerParams(vmem_limit_bytes=8 * 1024 * 1024),
    )(picks, back, d_gate, d_up, d_down)


def solution(mesh):
    spread = P(("dp", "expert"), None)
    weight = P("expert", "dp", None)
    return jax.shard_map(
        functools.partial(shards, mesh.shape["dp"], mesh.shape["expert"]),
        mesh=mesh,
        in_specs=(spread,) * 4 + (weight,) * 3,
        out_specs=(spread,) + (weight,) * 3,
        check_vma=False,
    )
```

```python
import functools

import jax
import jax.numpy as jnp
from jax import lax
from jax.experimental import pallas as pl
from jax.experimental.pallas import tpu as pltpu
from jax.sharding import PartitionSpec as P

LANES = 128
BF16 = jnp.bfloat16
F32 = jnp.float32
NT = (((1,), (1,)), ((), ()))


def block_of(hidden_units):
    return max(d for d in range(16, 177, 16) if hidden_units % d == 0)


def bulk_wait(ref, count, sem):
    part = ref.at[pl.ds(0, count)]
    pltpu.make_async_copy(part, part, sem).wait()


def exchange_kernel(
    n_dp,
    n_ex,
    picks_ref,
    gates_ref,
    tokens_hbm,
    cot_hbm,
    wg_hbm,
    wu_hbm,
    wd_hbm,
    back_out,
    gate_out,
    up_out,
    down_out,
    x_out,
    dy_out,
    dt_out,
    tok,
    cot,
    wg,
    wu,
    wd,
    wide,
    xmsg,
    dymsg,
    xbuf,
    dybuf,
    partmsg,
    backbuf,
    load_sem,
    send_sem,
    recv_sem,
):
    n = n_dp * n_ex
    experts, _, width = wg.shape
    chunks = width // LANES
    picked = picks_ref.shape[1]
    token_rows = tok.shape[0]
    my_dp, my_ex = lax.axis_index("dp"), lax.axis_index("expert")
    cores = 2
    n_chip = n // cores
    my_core, my_half = lax.rem(my_dp, cores), my_dp // cores
    my_chip = my_half * n_ex + my_ex
    me = my_core * n_chip + my_chip

    loads = [
        pltpu.make_async_copy(src, dst, load_sem.at[i])
        for i, (src, dst) in enumerate(
            ((tokens_hbm, tok), (cot_hbm, cot), (wg_hbm, wg), (wu_hbm, wu), (wd_hbm, wd))
        )
    ]
    for load in loads:
        load.start()

    def wrap(value, size):
        return jnp.where(value >= size, value - size, value)

    experts_at = [wrap(my_ex + b, n_ex) for b in range(n_ex)]

    def each_chip(act):
        for b in range(1, n_ex):
            act(my_half, experts_at[b])

        def ring(a, carry):
            half = wrap(my_half + a, n_dp // cores)
            for b in range(n_ex):
                act(half, experts_at[b])
            return carry

        lax.fori_loop(1, n_dp // cores, ring, 0)

    sibling = (my_half * cores + 1 - my_core, my_ex)

    barrier = pltpu.get_barrier_semaphore()

    def greet(where):
        pl.semaphore_signal(
            barrier, inc=1, device_id=where, device_id_type=pl.DeviceIdType.MESH
        )

    def greet_chip(half, ex):
        for core in range(cores):
            greet((half * cores + core, ex))

    greet(sibling)
    each_chip(greet_chip)

    eye = lax.broadcasted_iota(jnp.int32, (picked, picked), 0) == lax.broadcasted_iota(
        jnp.int32, (picked, picked), 1
    )
    pick_col = jnp.sum(
        jnp.where(eye, picks_ref[...].astype(F32), 0.0), axis=1, keepdims=True
    ).astype(jnp.int32)
    gate_col = jnp.sum(jnp.where(eye, gates_ref[...], 0.0), axis=1, keepdims=True)
    selector = jnp.where(
        lax.broadcasted_iota(jnp.int32, (picked, token_rows), 1) == pick_col, 1.0, 0.0
    ).astype(BF16)

    def pack(parts, msg):
        count = parts[0].shape[0]
        stride = len(parts) * chunks
        for e, value in enumerate(parts):
            for k in range(chunks):
                wide[pl.ds(e * chunks + k, count, stride=stride), :] = value[
                    :, k * LANES : (k + 1) * LANES
                ]
        msg[...] = wide[pl.ds(0, count * stride), :].astype(BF16).reshape(msg.shape)

    def unpack(buf, out):
        wide[...] = buf[...].reshape(wide.shape).astype(F32)
        for e in range(experts):
            for k in range(chunks):
                out[e, :, k * LANES : (k + 1) * LANES] = wide[
                    pl.ds(e * chunks + k, n, stride=experts * chunks), :
                ].astype(BF16)

    def remote(src, dst, slot, where):
        return pltpu.make_async_remote_copy(
            src_ref=src,
            dst_ref=dst,
            send_sem=send_sem.at[slot],
            recv_sem=recv_sem.at[slot],
            device_id=where,
            device_id_type=pl.DeviceIdType.MESH,
        )

    def send_chips(msg, buf, slot):
        def one(half, ex):
            where = (half * cores + my_core, ex)
            remote(msg.at[ex], buf.at[my_core, my_chip], slot, where).start()

        each_chip(one)
        buf[my_core, my_chip] = msg[my_ex]

    def hand_over(buf, slot):
        bulk_wait(buf.at[0], n_chip - 1, recv_sem.at[slot])
        copy = remote(buf.at[my_core], buf.at[my_core], slot + 1, sibling)
        copy.start()
        return copy

    def send_back(msg, buf, slot):
        def one(half, ex):
            for core in range(cores):
                spot = core * n_chip + half * n_ex + ex
                remote(msg.at[spot], buf.at[me], slot, (half * cores + core, ex)).start()

        each_chip(one)
        remote(msg.at[(1 - my_core) * n_chip + my_chip], buf.at[me], slot, sibling).start()
        buf[me] = msg[me]

    loads[0].wait()
    pack([jnp.dot(selector, tok[...], preferred_element_type=F32)], xmsg)
    pl.semaphore_wait(barrier, n - 1)
    send_chips(xmsg, xbuf, 0)
    loads[1].wait()
    pack([jnp.dot(selector, cot[...], preferred_element_type=F32) * gate_col], dymsg)
    send_chips(dymsg, dybuf, 2)

    def forward(e, value, weights):
        return lax.dot_general(value[e], weights[e], NT, preferred_element_type=F32)

    every = range(experts)
    x_copy = hand_over(xbuf, 0)
    x_copy.wait()
    unpack(xbuf, x_out)
    loads[2].wait()
    pre_gate = [forward(e, x_out, wg) for e in every]
    loads[3].wait()
    dy_copy = hand_over(dybuf, 2)
    pre_up = [forward(e, x_out, wu) for e in every]
    sigmoid_g = [jax.nn.sigmoid(g) for g in pre_gate]
    active = [g * s for g, s in zip(pre_gate, sigmoid_g)]
    slope = [
        u * s * (1.0 + g * (1.0 - s)) for g, u, s in zip(pre_gate, pre_up, sigmoid_g)
    ]
    for e in every:
        dt_out[e, 2] = (active[e] * pre_up[e]).T.astype(BF16)
    loads[4].wait()
    dy_copy.wait()
    unpack(dybuf, dy_out)
    grad_hidden = [forward(e, dy_out, wd) for e in every]
    d_up = [h * a for h, a in zip(grad_hidden, active)]
    d_gate = [h * s for h, s in zip(grad_hidden, slope)]
    pack(
        [
            jnp.dot(d_gate[e].astype(BF16), wg[e], preferred_element_type=F32)
            + jnp.dot(d_up[e].astype(BF16), wu[e], preferred_element_type=F32)
            for e in every
        ],
        partmsg,
    )
    send_back(partmsg, backbuf, 4)
    hidden_units = wg.shape[1]
    block = block_of(hidden_units)
    for e in every:
        dt_out[e, 0] = d_gate[e].T.astype(BF16)
        dt_out[e, 1] = d_up[e].T.astype(BF16)

        def grads(i, carry):
            at = pl.ds(pl.multiple_of(i * block, block), block)
            for j, (out, other) in enumerate(
                ((gate_out, x_out), (up_out, x_out), (down_out, dy_out))
            ):
                out[e, at, :] = jnp.dot(
                    dt_out[e, j, at, :], other[e], preferred_element_type=F32
                ).astype(BF16)
            return carry

        lax.fori_loop(0, hidden_units // block, grads, 0)
    bulk_wait(backbuf, n - 1, recv_sem.at[4])
    unpack(backbuf, back_out)
    bulk_wait(xbuf.at[0], n_chip - 1, send_sem.at[0])
    bulk_wait(dybuf.at[0], n_chip - 1, send_sem.at[2])
    bulk_wait(partmsg, n - 1, send_sem.at[4])


def store_kernel(
    n_dp,
    n_ex,
    picks_ref,
    back_hbm,
    gate_in,
    up_in,
    down_in,
    tokens_out,
    gate_out,
    up_out,
    down_out,
    back,
    total,
    sem,
    store_sem,
):
    load = pltpu.make_async_copy(back_hbm, back, sem.at[0])
    load.start()
    experts, hidden_units, _ = gate_in.shape
    half = hidden_units // 2 // 16 * 16
    stores = []
    for e in range(experts):
        for src, dst in ((gate_in, gate_out), (up_in, up_out), (down_in, down_out)):
            for at in (pl.ds(0, half), pl.ds(half, hidden_units - half)):
                stores.append(
                    pltpu.make_async_copy(
                        src.at[e, at], dst.at[e, at], store_sem.at[len(stores)]
                    )
                )
                stores[-1].start()
    token_rows = total.shape[0]
    picks = picks_ref[...].astype(F32)
    load.wait()
    columns = lax.broadcasted_iota(jnp.int32, (picks.shape[1], n_dp * n_ex), 0)
    places = lax.broadcasted_iota(jnp.int32, (picks.shape[1], n_dp * n_ex), 1)
    summed = jnp.zeros(total.shape, F32)
    for e in range(experts):
        wanted = jnp.where(columns == lax.rem(places, n_ex) * experts + e, 1.0, 0.0)
        row = jnp.dot(
            jnp.broadcast_to(picks, (8, picks.shape[1])).astype(BF16),
            wanted.astype(BF16),
            preferred_element_type=F32,
        )[:1]
        chosen = jnp.where(
            lax.broadcasted_iota(jnp.int32, (token_rows, n_dp * n_ex), 0).astype(F32) == row,
            1.0,
            0.0,
        ).astype(BF16)
        summed += jnp.dot(chosen, back[e], preferred_element_type=F32)
    total[...] = summed.astype(BF16)
    stores.append(pltpu.make_async_copy(total, tokens_out, sem.at[1]))
    stores[-1].start()
    for store in stores:
        store.wait()


def shards(n_dp, n_ex, tokens, cotangent, picks, gates, w_gate, w_up, w_down):
    picks, gates, tokens, cotangent, w_gate, w_up, w_down = (
        pltpu.with_memory_space_constraint(a, pltpu.HBM)
        for a in (picks, gates, tokens, cotangent, w_gate, w_up, w_down)
    )
    token_rows, width = tokens.shape
    experts, hidden, _ = w_gate.shape
    n = n_dp * n_ex
    rows = (experts, n, width)
    message = (experts * width // LANES, LANES)
    weight = pltpu.VMEM((experts, hidden, width), BF16)
    vmem = pl.BlockSpec(memory_space=pltpu.VMEM)
    anywhere = pl.BlockSpec(memory_space=pl.ANY)
    back, d_gate, d_up, d_down = pl.pallas_call(
        functools.partial(exchange_kernel, n_dp, n_ex),
        out_shape=(pltpu.VMEM(rows, BF16),) + (weight,) * 3,
        in_specs=[vmem] * 2 + [anywhere] * 5,
        out_specs=(vmem,) * 4,
        scratch_shapes=[
            pltpu.VMEM(rows, BF16),
            pltpu.VMEM(rows, BF16),
            pltpu.VMEM((experts, 3, hidden, n), BF16),
            pltpu.VMEM((token_rows, width), BF16),
            pltpu.VMEM((token_rows, width), BF16),
            weight,
            weight,
            weight,
            pltpu.VMEM((n * experts * width // LANES, LANES), F32),
            pltpu.VMEM((n_ex,) + message, BF16),
            pltpu.VMEM((n_ex,) + message, BF16),
            pltpu.VMEM((2, n // 2) + message, BF16),
            pltpu.VMEM((2, n // 2) + message, BF16),
            pltpu.VMEM((n,) + message, BF16),
            pltpu.VMEM((n,) + message, BF16),
            pltpu.SemaphoreType.DMA((5,)),
            pltpu.SemaphoreType.DMA((5,)),
            pltpu.SemaphoreType.DMA((5,)),
        ],
        compiler_params=pltpu.CompilerParams(
            collective_id=0, has_side_effects=True, vmem_limit_bytes=28 * 1024 * 1024
        ),
    )(picks, gates, tokens, cotangent, w_gate, w_up, w_down)

    grad = jax.ShapeDtypeStruct(w_gate.shape, BF16)
    return pl.pallas_call(
        functools.partial(store_kernel, n_dp, n_ex),
        out_shape=(jax.ShapeDtypeStruct(tokens.shape, BF16), grad, grad, grad),
        in_specs=[vmem] + [anywhere] * 4,
        out_specs=(anywhere,) * 4,
        scratch_shapes=[
            pltpu.VMEM(rows, BF16),
            pltpu.VMEM(tokens.shape, BF16),
            pltpu.SemaphoreType.DMA((2,)),
            pltpu.SemaphoreType.DMA((6 * experts,)),
        ],
        compiler_params=pltpu.CompilerParams(vmem_limit_bytes=8 * 1024 * 1024),
    )(picks, back, d_gate, d_up, d_down)


def solution(mesh):
    spread = P(("dp", "expert"), None)
    weight = P("expert", "dp", None)
    return jax.shard_map(
        functools.partial(shards, mesh.shape["dp"], mesh.shape["expert"]),
        mesh=mesh,
        in_specs=(spread,) * 4 + (weight,) * 3,
        out_specs=(spread,) + (weight,) * 3,
        check_vma=False,
    )
```

```python
import functools

import jax
import jax.numpy as jnp
from jax import lax
from jax.experimental import pallas as pl
from jax.experimental.pallas import tpu as pltpu
from jax.sharding import PartitionSpec as P

LANES = 128
BF16 = jnp.bfloat16
F32 = jnp.float32
NT = (((1,), (1,)), ((), ()))


def block_of(hidden_units):
    return max(d for d in range(16, 177, 16) if hidden_units % d == 0)


def bulk_wait(ref, count, sem):
    part = ref.at[pl.ds(0, count)]
    pltpu.make_async_copy(part, part, sem).wait()


def exchange_kernel(
    n_dp,
    n_ex,
    picks_ref,
    gates_ref,
    tokens_hbm,
    cot_hbm,
    wg_hbm,
    wu_hbm,
    wd_hbm,
    back_out,
    gate_out,
    up_out,
    down_out,
    x_out,
    dy_out,
    dt_out,
    tok,
    cot,
    wg,
    wu,
    wd,
    wide,
    xmsg,
    dymsg,
    xbuf,
    dybuf,
    partmsg,
    backbuf,
    load_sem,
    send_sem,
    recv_sem,
):
    n = n_dp * n_ex
    experts, _, width = wg.shape
    chunks = width // LANES
    picked = picks_ref.shape[1]
    token_rows = tok.shape[0]
    my_dp, my_ex = lax.axis_index("dp"), lax.axis_index("expert")
    cores = 2
    n_chip = n // cores
    my_core, my_half = lax.rem(my_dp, cores), my_dp // cores
    my_chip = my_half * n_ex + my_ex
    me = my_core * n_chip + my_chip

    loads = [
        pltpu.make_async_copy(src, dst, load_sem.at[i])
        for i, (src, dst) in enumerate(
            ((tokens_hbm, tok), (cot_hbm, cot), (wg_hbm, wg), (wu_hbm, wu), (wd_hbm, wd))
        )
    ]
    for load in loads:
        load.start()

    def wrap(value, size):
        return jnp.where(value >= size, value - size, value)

    experts_at = [wrap(my_ex + b, n_ex) for b in range(n_ex)]

    def each_chip(act):
        for b in range(1, n_ex):
            act(my_half, experts_at[b])

        def ring(a, carry):
            half = wrap(my_half + a, n_dp // cores)
            for b in range(n_ex):
                act(half, experts_at[b])
            return carry

        lax.fori_loop(1, n_dp // cores, ring, 0)

    sibling = (my_half * cores + 1 - my_core, my_ex)

    barrier = pltpu.get_barrier_semaphore()

    def greet(where):
        pl.semaphore_signal(
            barrier, inc=1, device_id=where, device_id_type=pl.DeviceIdType.MESH
        )

    def greet_chip(half, ex):
        for core in range(cores):
            greet((half * cores + core, ex))

    greet(sibling)
    each_chip(greet_chip)

    eye = lax.broadcasted_iota(jnp.int32, (picked, picked), 0) == lax.broadcasted_iota(
        jnp.int32, (picked, picked), 1
    )
    pick_col = jnp.sum(
        jnp.where(eye, picks_ref[...].astype(F32), 0.0), axis=1, keepdims=True
    ).astype(jnp.int32)
    gate_col = jnp.sum(jnp.where(eye, gates_ref[...], 0.0), axis=1, keepdims=True)
    selector = jnp.where(
        lax.broadcasted_iota(jnp.int32, (picked, token_rows), 1) == pick_col, 1.0, 0.0
    ).astype(BF16)

    def pack(parts, msg):
        count = parts[0].shape[0]
        stride = len(parts) * chunks
        for e, value in enumerate(parts):
            for k in range(chunks):
                wide[pl.ds(e * chunks + k, count, stride=stride), :] = value[
                    :, k * LANES : (k + 1) * LANES
                ]
        msg[...] = wide[pl.ds(0, count * stride), :].astype(BF16).reshape(msg.shape)

    def unpack(buf, out):
        wide[...] = buf[...].reshape(wide.shape).astype(F32)
        for e in range(experts):
            for k in range(chunks):
                out[e, :, k * LANES : (k + 1) * LANES] = wide[
                    pl.ds(e * chunks + k, n, stride=experts * chunks), :
                ].astype(BF16)

    def remote(src, dst, slot, where):
        return pltpu.make_async_remote_copy(
            src_ref=src,
            dst_ref=dst,
            send_sem=send_sem.at[slot],
            recv_sem=recv_sem.at[slot],
            device_id=where,
            device_id_type=pl.DeviceIdType.MESH,
        )

    def send_chips(msg, buf, slot):
        def one(half, ex):
            where = (half * cores + my_core, ex)
            remote(msg.at[ex], buf.at[my_core, my_chip], slot, where).start()

        each_chip(one)
        buf[my_core, my_chip] = msg[my_ex]

    def hand_over(buf, slot):
        bulk_wait(buf.at[0], n_chip - 1, recv_sem.at[slot])
        copy = remote(buf.at[my_core], buf.at[my_core], slot + 1, sibling)
        copy.start()
        return copy

    def send_back(msg, buf, slot):
        def one(half, ex):
            for core in range(cores):
                spot = core * n_chip + half * n_ex + ex
                remote(msg.at[spot], buf.at[me], slot, (half * cores + core, ex)).start()

        each_chip(one)
        remote(msg.at[(1 - my_core) * n_chip + my_chip], buf.at[me], slot, sibling).start()
        buf[me] = msg[me]

    loads[0].wait()
    pack([jnp.dot(selector, tok[...], preferred_element_type=F32)], xmsg)
    pl.semaphore_wait(barrier, n - 1)
    send_chips(xmsg, xbuf, 0)
    loads[1].wait()
    pack([jnp.dot(selector, cot[...], preferred_element_type=F32) * gate_col], dymsg)
    send_chips(dymsg, dybuf, 2)

    def forward(e, value, weights):
        return lax.dot_general(weights[e], value[e], NT, preferred_element_type=F32).T

    every = range(experts)
    x_copy = hand_over(xbuf, 0)
    x_copy.wait()
    unpack(xbuf, x_out)
    loads[2].wait()
    pre_gate = [forward(e, x_out, wg) for e in every]
    loads[3].wait()
    dy_copy = hand_over(dybuf, 2)
    pre_up = [forward(e, x_out, wu) for e in every]
    sigmoid_g = [jax.nn.sigmoid(g) for g in pre_gate]
    active = [g * s for g, s in zip(pre_gate, sigmoid_g)]
    slope = [
        u * s * (1.0 + g * (1.0 - s)) for g, u, s in zip(pre_gate, pre_up, sigmoid_g)
    ]
    for e in every:
        dt_out[e, 2] = (active[e] * pre_up[e]).T.astype(BF16)
    loads[4].wait()
    dy_copy.wait()
    unpack(dybuf, dy_out)
    grad_hidden = [forward(e, dy_out, wd) for e in every]
    d_up = [h * a for h, a in zip(grad_hidden, active)]
    d_gate = [h * s for h, s in zip(grad_hidden, slope)]
    pack(
        [
            jnp.dot(d_gate[e].astype(BF16), wg[e], preferred_element_type=F32)
            + jnp.dot(d_up[e].astype(BF16), wu[e], preferred_element_type=F32)
            for e in every
        ],
        partmsg,
    )
    send_back(partmsg, backbuf, 4)
    hidden_units = wg.shape[1]
    block = block_of(hidden_units)
    for e in every:
        dt_out[e, 0] = d_gate[e].T.astype(BF16)
        dt_out[e, 1] = d_up[e].T.astype(BF16)

        def grads(i, carry):
            at = pl.ds(pl.multiple_of(i * block, block), block)
            for j, (out, other) in enumerate(
                ((gate_out, x_out), (up_out, x_out), (down_out, dy_out))
            ):
                out[e, at, :] = jnp.dot(
                    dt_out[e, j, at, :], other[e], preferred_element_type=F32
                ).astype(BF16)
            return carry

        lax.fori_loop(0, hidden_units // block, grads, 0)
    bulk_wait(backbuf, n - 1, recv_sem.at[4])
    unpack(backbuf, back_out)
    bulk_wait(xbuf.at[0], n_chip - 1, send_sem.at[0])
    bulk_wait(dybuf.at[0], n_chip - 1, send_sem.at[2])
    bulk_wait(partmsg, n - 1, send_sem.at[4])


def store_kernel(
    n_dp,
    n_ex,
    picks_ref,
    back_hbm,
    gate_in,
    up_in,
    down_in,
    tokens_out,
    gate_out,
    up_out,
    down_out,
    back,
    total,
    sem,
    store_sem,
):
    load = pltpu.make_async_copy(back_hbm, back, sem.at[0])
    load.start()
    experts, hidden_units, _ = gate_in.shape
    half = hidden_units // 2 // 16 * 16
    stores = []
    for e in range(experts):
        for src, dst in ((gate_in, gate_out), (up_in, up_out), (down_in, down_out)):
            for at in (pl.ds(0, half), pl.ds(half, hidden_units - half)):
                stores.append(
                    pltpu.make_async_copy(
                        src.at[e, at], dst.at[e, at], store_sem.at[len(stores)]
                    )
                )
                stores[-1].start()
    token_rows = total.shape[0]
    picks = picks_ref[...].astype(F32)
    load.wait()
    columns = lax.broadcasted_iota(jnp.int32, (picks.shape[1], n_dp * n_ex), 0)
    places = lax.broadcasted_iota(jnp.int32, (picks.shape[1], n_dp * n_ex), 1)
    summed = jnp.zeros(total.shape, F32)
    for e in range(experts):
        wanted = jnp.where(columns == lax.rem(places, n_ex) * experts + e, 1.0, 0.0)
        row = jnp.dot(
            jnp.broadcast_to(picks, (8, picks.shape[1])).astype(BF16),
            wanted.astype(BF16),
            preferred_element_type=F32,
        )[:1]
        chosen = jnp.where(
            lax.broadcasted_iota(jnp.int32, (token_rows, n_dp * n_ex), 0).astype(F32) == row,
            1.0,
            0.0,
        ).astype(BF16)
        summed += jnp.dot(chosen, back[e], preferred_element_type=F32)
    total[...] = summed.astype(BF16)
    stores.append(pltpu.make_async_copy(total, tokens_out, sem.at[1]))
    stores[-1].start()
    for store in stores:
        store.wait()


def shards(n_dp, n_ex, tokens, cotangent, picks, gates, w_gate, w_up, w_down):
    picks, gates, tokens, cotangent, w_gate, w_up, w_down = (
        pltpu.with_memory_space_constraint(a, pltpu.HBM)
        for a in (picks, gates, tokens, cotangent, w_gate, w_up, w_down)
    )
    token_rows, width = tokens.shape
    experts, hidden, _ = w_gate.shape
    n = n_dp * n_ex
    rows = (experts, n, width)
    message = (experts * width // LANES, LANES)
    weight = pltpu.VMEM((experts, hidden, width), BF16)
    vmem = pl.BlockSpec(memory_space=pltpu.VMEM)
    anywhere = pl.BlockSpec(memory_space=pl.ANY)
    back, d_gate, d_up, d_down = pl.pallas_call(
        functools.partial(exchange_kernel, n_dp, n_ex),
        out_shape=(pltpu.VMEM(rows, BF16),) + (weight,) * 3,
        in_specs=[vmem] * 2 + [anywhere] * 5,
        out_specs=(vmem,) * 4,
        scratch_shapes=[
            pltpu.VMEM(rows, BF16),
            pltpu.VMEM(rows, BF16),
            pltpu.VMEM((experts, 3, hidden, n), BF16),
            pltpu.VMEM((token_rows, width), BF16),
            pltpu.VMEM((token_rows, width), BF16),
            weight,
            weight,
            weight,
            pltpu.VMEM((n * experts * width // LANES, LANES), F32),
            pltpu.VMEM((n_ex,) + message, BF16),
            pltpu.VMEM((n_ex,) + message, BF16),
            pltpu.VMEM((2, n // 2) + message, BF16),
            pltpu.VMEM((2, n // 2) + message, BF16),
            pltpu.VMEM((n,) + message, BF16),
            pltpu.VMEM((n,) + message, BF16),
            pltpu.SemaphoreType.DMA((5,)),
            pltpu.SemaphoreType.DMA((5,)),
            pltpu.SemaphoreType.DMA((5,)),
        ],
        compiler_params=pltpu.CompilerParams(
            collective_id=0, has_side_effects=True, vmem_limit_bytes=28 * 1024 * 1024
        ),
    )(picks, gates, tokens, cotangent, w_gate, w_up, w_down)

    grad = jax.ShapeDtypeStruct(w_gate.shape, BF16)
    return pl.pallas_call(
        functools.partial(store_kernel, n_dp, n_ex),
        out_shape=(jax.ShapeDtypeStruct(tokens.shape, BF16), grad, grad, grad),
        in_specs=[vmem] + [anywhere] * 4,
        out_specs=(anywhere,) * 4,
        scratch_shapes=[
            pltpu.VMEM(rows, BF16),
            pltpu.VMEM(tokens.shape, BF16),
            pltpu.SemaphoreType.DMA((2,)),
            pltpu.SemaphoreType.DMA((6 * experts,)),
        ],
        compiler_params=pltpu.CompilerParams(vmem_limit_bytes=8 * 1024 * 1024),
    )(picks, back, d_gate, d_up, d_down)


def solution(mesh):
    spread = P(("dp", "expert"), None)
    weight = P("expert", "dp", None)
    return jax.shard_map(
        functools.partial(shards, mesh.shape["dp"], mesh.shape["expert"]),
        mesh=mesh,
        in_specs=(spread,) * 4 + (weight,) * 3,
        out_specs=(spread,) + (weight,) * 3,
        check_vma=False,
    )
```

```python
import functools

import jax
import jax.numpy as jnp
from jax import lax
from jax.experimental import pallas as pl
from jax.experimental.pallas import tpu as pltpu
from jax.sharding import PartitionSpec as P

LANES = 128
BF16 = jnp.bfloat16
F32 = jnp.float32
NT = (((1,), (1,)), ((), ()))


def block_of(hidden_units):
    return max(d for d in range(16, 177, 16) if hidden_units % d == 0)


def bulk_wait(ref, count, sem):
    part = ref.at[pl.ds(0, count)]
    pltpu.make_async_copy(part, part, sem).wait()


def unpack(buf, wide, out):
    experts, n, width = out.shape
    chunks = width // LANES
    wide[...] = buf[...].reshape(wide.shape).astype(F32)
    for e in range(experts):
        for k in range(chunks):
            out[e, :, k * LANES : (k + 1) * LANES] = wide[
                pl.ds(e * chunks + k, n, stride=experts * chunks), :
            ].astype(BF16)


def exchange_kernel(
    n_dp,
    n_ex,
    picks_hbm,
    gates_hbm,
    tokens_hbm,
    cot_hbm,
    wg_hbm,
    wu_hbm,
    wd_hbm,
    back_out,
    gate_out,
    up_out,
    down_out,
    x_out,
    dy_out,
    dt_out,
    picks_ref,
    gates_ref,
    tok,
    cot,
    wg,
    wu,
    wd,
    wide,
    xmsg,
    dymsg,
    xbuf,
    dybuf,
    partmsg,
    backbuf,
    load_sem,
    send_sem,
    recv_sem,
):
    n = n_dp * n_ex
    experts, _, width = wg.shape
    chunks = width // LANES
    picked = picks_ref.shape[1]
    token_rows = tok.shape[0]
    my_dp, my_ex = lax.axis_index("dp"), lax.axis_index("expert")
    cores = 2
    n_chip = n // cores
    my_core, my_half = lax.rem(my_dp, cores), my_dp // cores
    my_chip = my_half * n_ex + my_ex
    me = my_core * n_chip + my_chip

    loads = [
        pltpu.make_async_copy(src, dst, load_sem.at[i])
        for i, (src, dst) in enumerate(
            (
                (picks_hbm, picks_ref),
                (tokens_hbm, tok),
                (gates_hbm, gates_ref),
                (cot_hbm, cot),
                (wg_hbm, wg),
                (wu_hbm, wu),
                (wd_hbm, wd),
            )
        )
    ]
    for load in loads:
        load.start()

    def wrap(value, size):
        return jnp.where(value >= size, value - size, value)

    experts_at = [wrap(my_ex + b, n_ex) for b in range(n_ex)]

    def each_chip(act):
        for b in range(1, n_ex):
            act(my_half, experts_at[b])

        def ring(a, carry):
            half = wrap(my_half + a, n_dp // cores)
            for b in range(n_ex):
                act(half, experts_at[b])
            return carry

        lax.fori_loop(1, n_dp // cores, ring, 0)

    sibling = (my_half * cores + 1 - my_core, my_ex)

    barrier = pltpu.get_barrier_semaphore()

    def greet(where):
        pl.semaphore_signal(
            barrier, inc=1, device_id=where, device_id_type=pl.DeviceIdType.MESH
        )

    def greet_chip(half, ex):
        for core in range(cores):
            greet((half * cores + core, ex))

    greet(sibling)
    each_chip(greet_chip)

    eye = lax.broadcasted_iota(jnp.int32, (picked, picked), 0) == lax.broadcasted_iota(
        jnp.int32, (picked, picked), 1
    )
    loads[0].wait()
    pick_col = jnp.sum(
        jnp.where(eye, picks_ref[...].astype(F32), 0.0), axis=1, keepdims=True
    ).astype(jnp.int32)
    selector = jnp.where(
        lax.broadcasted_iota(jnp.int32, (picked, token_rows), 1) == pick_col, 1.0, 0.0
    ).astype(BF16)

    def pack(parts, msg):
        count = parts[0].shape[0]
        stride = len(parts) * chunks
        for e, value in enumerate(parts):
            for k in range(chunks):
                wide[pl.ds(e * chunks + k, count, stride=stride), :] = value[
                    :, k * LANES : (k + 1) * LANES
                ]
        msg[...] = wide[pl.ds(0, count * stride), :].astype(BF16).reshape(msg.shape)

    def remote(src, dst, slot, where):
        return pltpu.make_async_remote_copy(
            src_ref=src,
            dst_ref=dst,
            send_sem=send_sem.at[slot],
            recv_sem=recv_sem.at[slot],
            device_id=where,
            device_id_type=pl.DeviceIdType.MESH,
        )

    def send_chips(msg, buf, slot):
        def one(half, ex):
            where = (half * cores + my_core, ex)
            remote(msg.at[ex], buf.at[my_core, my_chip], slot, where).start()

        each_chip(one)
        buf[my_core, my_chip] = msg[my_ex]

    def hand_over(buf, slot):
        bulk_wait(buf.at[0], n_chip - 1, recv_sem.at[slot])
        copy = remote(buf.at[my_core], buf.at[my_core], slot + 1, sibling)
        copy.start()
        return copy

    def send_back(msg, buf, slot):
        def one(half, ex):
            for core in range(cores):
                spot = core * n_chip + half * n_ex + ex
                remote(msg.at[spot], buf.at[me], slot, (half * cores + core, ex)).start()

        each_chip(one)
        remote(msg.at[(1 - my_core) * n_chip + my_chip], buf.at[me], slot, sibling).start()
        buf[me] = msg[me]

    loads[1].wait()
    pack([jnp.dot(selector, tok[...], preferred_element_type=F32)], xmsg)
    pl.semaphore_wait(barrier, n - 1)
    send_chips(xmsg, xbuf, 0)
    loads[2].wait()
    gate_col = jnp.sum(jnp.where(eye, gates_ref[...], 0.0), axis=1, keepdims=True)
    loads[3].wait()
    pack([jnp.dot(selector, cot[...], preferred_element_type=F32) * gate_col], dymsg)
    send_chips(dymsg, dybuf, 2)

    def forward(e, value, weights):
        return lax.dot_general(value[e], weights[e], NT, preferred_element_type=F32)

    every = range(experts)
    x_copy = hand_over(xbuf, 0)
    x_copy.wait()
    unpack(xbuf, wide, x_out)
    loads[4].wait()
    pre_gate = [forward(e, x_out, wg) for e in every]
    loads[5].wait()
    dy_copy = hand_over(dybuf, 2)
    pre_up = [forward(e, x_out, wu) for e in every]
    sigmoid_g = [jax.nn.sigmoid(g) for g in pre_gate]
    active = [g * s for g, s in zip(pre_gate, sigmoid_g)]
    slope = [
        u * s * (1.0 + g * (1.0 - s)) for g, u, s in zip(pre_gate, pre_up, sigmoid_g)
    ]
    hidden = [a * u for a, u in zip(active, pre_up)]
    loads[6].wait()
    dy_copy.wait()
    unpack(dybuf, wide, dy_out)
    grad_hidden = [forward(e, dy_out, wd) for e in every]
    d_up = [h * a for h, a in zip(grad_hidden, active)]
    d_gate = [h * s for h, s in zip(grad_hidden, slope)]
    pack(
        [
            jnp.dot(d_gate[e].astype(BF16), wg[e], preferred_element_type=F32)
            + jnp.dot(d_up[e].astype(BF16), wu[e], preferred_element_type=F32)
            for e in every
        ],
        partmsg,
    )
    send_back(partmsg, backbuf, 4)
    hidden_units = wg.shape[1]
    block = block_of(hidden_units)
    for e in every:
        dt_out[e, 0] = d_gate[e].T.astype(BF16)
        dt_out[e, 1] = d_up[e].T.astype(BF16)
        dt_out[e, 2] = hidden[e].T.astype(BF16)

        def grads(i, carry):
            at = pl.ds(pl.multiple_of(i * block, block), block)
            for j, (out, other) in enumerate(
                ((gate_out, x_out), (up_out, x_out), (down_out, dy_out))
            ):
                out[e, at, :] = jnp.dot(
                    dt_out[e, j, at, :], other[e], preferred_element_type=F32
                ).astype(BF16)
            return carry

        lax.fori_loop(0, hidden_units // block, grads, 0)
    bulk_wait(backbuf, n - 1, recv_sem.at[4])
    back_out[...] = backbuf[...]
    bulk_wait(xbuf.at[0], n_chip - 1, send_sem.at[0])
    bulk_wait(dybuf.at[0], n_chip - 1, send_sem.at[2])
    bulk_wait(partmsg, n - 1, send_sem.at[4])


def store_kernel(
    n_dp,
    n_ex,
    picks_hbm,
    back_in,
    gate_in,
    up_in,
    down_in,
    tokens_out,
    gate_out,
    up_out,
    down_out,
    picks_ref,
    raw,
    wide,
    back,
    total,
    sem,
    store_sem,
):
    picks_load = pltpu.make_async_copy(picks_hbm, picks_ref, sem.at[0])
    picks_load.start()
    load = pltpu.make_async_copy(back_in, raw, sem.at[2])
    load.start()
    experts, hidden_units, _ = gate_in.shape
    half = hidden_units // 2 // 16 * 16
    stores = []
    for e in range(experts):
        for src, dst in ((gate_in, gate_out), (up_in, up_out), (down_in, down_out)):
            for at in (pl.ds(0, half), pl.ds(half, hidden_units - half)):
                stores.append(
                    pltpu.make_async_copy(
                        src.at[e, at], dst.at[e, at], store_sem.at[len(stores)]
                    )
                )
                stores[-1].start()
    token_rows = total.shape[0]
    load.wait()
    unpack(raw, wide, back)
    picks_load.wait()
    picks = picks_ref[...].astype(F32)
    columns = lax.broadcasted_iota(jnp.int32, (picks.shape[1], n_dp * n_ex), 0)
    places = lax.broadcasted_iota(jnp.int32, (picks.shape[1], n_dp * n_ex), 1)
    summed = jnp.zeros(total.shape, F32)
    for e in range(experts):
        wanted = jnp.where(columns == lax.rem(places, n_ex) * experts + e, 1.0, 0.0)
        row = jnp.dot(
            jnp.broadcast_to(picks, (8, picks.shape[1])).astype(BF16),
            wanted.astype(BF16),
            preferred_element_type=F32,
        )[:1]
        chosen = jnp.where(
            lax.broadcasted_iota(jnp.int32, (token_rows, n_dp * n_ex), 0).astype(F32) == row,
            1.0,
            0.0,
        ).astype(BF16)
        summed += jnp.dot(chosen, back[e], preferred_element_type=F32)
    total[...] = summed.astype(BF16)
    stores.append(pltpu.make_async_copy(total, tokens_out, sem.at[1]))
    stores[-1].start()
    for store in stores:
        store.wait()


def shards(n_dp, n_ex, tokens, cotangent, picks, gates, w_gate, w_up, w_down):
    picks, gates, tokens, cotangent, w_gate, w_up, w_down = (
        pltpu.with_memory_space_constraint(a, pltpu.HBM)
        for a in (picks, gates, tokens, cotangent, w_gate, w_up, w_down)
    )
    token_rows, width = tokens.shape
    experts, hidden, _ = w_gate.shape
    n = n_dp * n_ex
    rows = (experts, n, width)
    message = (experts * width // LANES, LANES)
    weight = pltpu.VMEM((experts, hidden, width), BF16)
    vmem = pl.BlockSpec(memory_space=pltpu.VMEM)
    anywhere = pl.BlockSpec(memory_space=pl.ANY)
    back, d_gate, d_up, d_down = pl.pallas_call(
        functools.partial(exchange_kernel, n_dp, n_ex),
        out_shape=(pltpu.VMEM((n,) + message, BF16),) + (weight,) * 3,
        in_specs=[anywhere] * 7,
        out_specs=(vmem,) * 4,
        scratch_shapes=[
            pltpu.VMEM(rows, BF16),
            pltpu.VMEM(rows, BF16),
            pltpu.VMEM((experts, 3, hidden, n), BF16),
            pltpu.VMEM(picks.shape, jnp.int32),
            pltpu.VMEM(gates.shape, F32),
            pltpu.VMEM((token_rows, width), BF16),
            pltpu.VMEM((token_rows, width), BF16),
            weight,
            weight,
            weight,
            pltpu.VMEM((n * experts * width // LANES, LANES), F32),
            pltpu.VMEM((n_ex,) + message, BF16),
            pltpu.VMEM((n_ex,) + message, BF16),
            pltpu.VMEM((2, n // 2) + message, BF16),
            pltpu.VMEM((2, n // 2) + message, BF16),
            pltpu.VMEM((n,) + message, BF16),
            pltpu.VMEM((n,) + message, BF16),
            pltpu.SemaphoreType.DMA((7,)),
            pltpu.SemaphoreType.DMA((5,)),
            pltpu.SemaphoreType.DMA((5,)),
        ],
        compiler_params=pltpu.CompilerParams(
            collective_id=0, has_side_effects=True, vmem_limit_bytes=28 * 1024 * 1024
        ),
    )(picks, gates, tokens, cotangent, w_gate, w_up, w_down)

    grad = jax.ShapeDtypeStruct(w_gate.shape, BF16)
    return pl.pallas_call(
        functools.partial(store_kernel, n_dp, n_ex),
        out_shape=(jax.ShapeDtypeStruct(tokens.shape, BF16), grad, grad, grad),
        in_specs=[anywhere] * 5,
        out_specs=(anywhere,) * 4,
        scratch_shapes=[
            pltpu.VMEM(picks.shape, jnp.int32),
            pltpu.VMEM((n,) + message, BF16),
            pltpu.VMEM((n * experts * width // LANES, LANES), F32),
            pltpu.VMEM(rows, BF16),
            pltpu.VMEM(tokens.shape, BF16),
            pltpu.SemaphoreType.DMA((3,)),
            pltpu.SemaphoreType.DMA((6 * experts,)),
        ],
        compiler_params=pltpu.CompilerParams(vmem_limit_bytes=16 * 1024 * 1024),
    )(picks, back, d_gate, d_up, d_down)


def solution(mesh):
    spread = P(("dp", "expert"), None)
    weight = P("expert", "dp", None)
    return jax.shard_map(
        functools.partial(shards, mesh.shape["dp"], mesh.shape["expert"]),
        mesh=mesh,
        in_specs=(spread,) * 4 + (weight,) * 3,
        out_specs=(spread,) + (weight,) * 3,
        check_vma=False,
    )
```

```python
import functools

import jax
import jax.numpy as jnp
from jax import lax
from jax.experimental import pallas as pl
from jax.experimental.pallas import tpu as pltpu
from jax.sharding import PartitionSpec as P

LANES = 128
BF16 = jnp.bfloat16
F32 = jnp.float32
NT = (((1,), (1,)), ((), ()))


def block_of(hidden_units):
    return max(d for d in range(16, 177, 16) if hidden_units % d == 0)


def bulk_wait(ref, count, sem):
    part = ref.at[pl.ds(0, count)]
    pltpu.make_async_copy(part, part, sem).wait()


def unpack(buf, wide, out):
    experts, n, width = out.shape
    chunks = width // LANES
    wide[...] = buf[...].reshape(wide.shape).astype(F32)
    for e in range(experts):
        for k in range(chunks):
            out[e, :, k * LANES : (k + 1) * LANES] = wide[
                pl.ds(e * chunks + k, n, stride=experts * chunks), :
            ].astype(BF16)


def exchange_kernel(
    n_dp,
    n_ex,
    picks_hbm,
    gates_hbm,
    tokens_hbm,
    cot_hbm,
    wg_hbm,
    wu_hbm,
    wd_hbm,
    back_out,
    gate_out,
    up_out,
    dy_out,
    hidden_out,
    x_out,
    dt_out,
    picks_ref,
    gates_ref,
    tok,
    cot,
    wg,
    wu,
    wd,
    wide,
    xmsg,
    dymsg,
    xbuf,
    dybuf,
    partmsg,
    backbuf,
    load_sem,
    send_sem,
    recv_sem,
):
    n = n_dp * n_ex
    experts, _, width = wg.shape
    chunks = width // LANES
    picked = picks_ref.shape[1]
    token_rows = tok.shape[0]
    my_dp, my_ex = lax.axis_index("dp"), lax.axis_index("expert")
    cores = 2
    n_chip = n // cores
    my_core, my_half = lax.rem(my_dp, cores), my_dp // cores
    my_chip = my_half * n_ex + my_ex
    me = my_core * n_chip + my_chip

    loads = [
        pltpu.make_async_copy(src, dst, load_sem.at[i])
        for i, (src, dst) in enumerate(
            (
                (picks_hbm, picks_ref),
                (tokens_hbm, tok),
                (gates_hbm, gates_ref),
                (cot_hbm, cot),
                (wg_hbm, wg),
                (wu_hbm, wu),
                (wd_hbm, wd),
            )
        )
    ]
    for load in loads[:4]:
        load.start()

    def wrap(value, size):
        return jnp.where(value >= size, value - size, value)

    experts_at = [wrap(my_ex + b, n_ex) for b in range(n_ex)]

    def each_chip(act):
        for b in range(1, n_ex):
            act(my_half, experts_at[b])

        def ring(a, carry):
            half = wrap(my_half + a, n_dp // cores)
            for b in range(n_ex):
                act(half, experts_at[b])
            return carry

        lax.fori_loop(1, n_dp // cores, ring, 0)

    sibling = (my_half * cores + 1 - my_core, my_ex)

    barrier = pltpu.get_barrier_semaphore()

    def greet(where):
        pl.semaphore_signal(
            barrier, inc=1, device_id=where, device_id_type=pl.DeviceIdType.MESH
        )

    def greet_chip(half, ex):
        for core in range(cores):
            greet((half * cores + core, ex))

    greet(sibling)
    each_chip(greet_chip)

    eye = lax.broadcasted_iota(jnp.int32, (picked, picked), 0) == lax.broadcasted_iota(
        jnp.int32, (picked, picked), 1
    )
    loads[0].wait()
    pick_col = jnp.sum(
        jnp.where(eye, picks_ref[...].astype(F32), 0.0), axis=1, keepdims=True
    ).astype(jnp.int32)
    selector = jnp.where(
        lax.broadcasted_iota(jnp.int32, (picked, token_rows), 1) == pick_col, 1.0, 0.0
    ).astype(BF16)

    def pack(parts, msg):
        count = parts[0].shape[0]
        stride = len(parts) * chunks
        for e, value in enumerate(parts):
            for k in range(chunks):
                wide[pl.ds(e * chunks + k, count, stride=stride), :] = value[
                    :, k * LANES : (k + 1) * LANES
                ]
        msg[...] = wide[pl.ds(0, count * stride), :].astype(BF16).reshape(msg.shape)

    def remote(src, dst, slot, where):
        return pltpu.make_async_remote_copy(
            src_ref=src,
            dst_ref=dst,
            send_sem=send_sem.at[slot],
            recv_sem=recv_sem.at[slot],
            device_id=where,
            device_id_type=pl.DeviceIdType.MESH,
        )

    def send_chips(msg, buf, slot):
        def one(half, ex):
            where = (half * cores + my_core, ex)
            remote(msg.at[ex], buf.at[my_core, my_chip], slot, where).start()

        each_chip(one)
        buf[my_core, my_chip] = msg[my_ex]

    def hand_over(buf, slot):
        bulk_wait(buf.at[0], n_chip - 1, recv_sem.at[slot])
        copy = remote(buf.at[my_core], buf.at[my_core], slot + 1, sibling)
        copy.start()
        return copy

    def send_back(msg, buf, slot):
        def one(half, ex):
            for core in range(cores):
                spot = core * n_chip + half * n_ex + ex
                remote(msg.at[spot], buf.at[me], slot, (half * cores + core, ex)).start()

        each_chip(one)
        remote(msg.at[(1 - my_core) * n_chip + my_chip], buf.at[me], slot, sibling).start()
        buf[me] = msg[me]

    loads[1].wait()
    for load in loads[4:]:
        load.start()
    pack([jnp.dot(selector, tok[...], preferred_element_type=F32)], xmsg)
    pl.semaphore_wait(barrier, n - 1)
    send_chips(xmsg, xbuf, 0)
    loads[2].wait()
    gate_col = jnp.sum(jnp.where(eye, gates_ref[...], 0.0), axis=1, keepdims=True)
    loads[3].wait()
    pack([jnp.dot(selector, cot[...], preferred_element_type=F32) * gate_col], dymsg)
    send_chips(dymsg, dybuf, 2)

    def forward(e, value, weights):
        return lax.dot_general(value[e], weights[e], NT, preferred_element_type=F32)

    every = range(experts)
    x_copy = hand_over(xbuf, 0)
    x_copy.wait()
    unpack(xbuf, wide, x_out)
    loads[4].wait()
    pre_gate = [forward(e, x_out, wg) for e in every]
    loads[5].wait()
    dy_copy = hand_over(dybuf, 2)
    pre_up = [forward(e, x_out, wu) for e in every]
    sigmoid_g = [jax.nn.sigmoid(g) for g in pre_gate]
    active = [g * s for g, s in zip(pre_gate, sigmoid_g)]
    slope = [
        u * s * (1.0 + g * (1.0 - s)) for g, u, s in zip(pre_gate, pre_up, sigmoid_g)
    ]
    hidden = [a * u for a, u in zip(active, pre_up)]
    loads[6].wait()
    dy_copy.wait()
    unpack(dybuf, wide, dy_out)
    grad_hidden = [forward(e, dy_out, wd) for e in every]
    d_up = [h * a for h, a in zip(grad_hidden, active)]
    d_gate = [h * s for h, s in zip(grad_hidden, slope)]
    pack(
        [
            jnp.dot(d_gate[e].astype(BF16), wg[e], preferred_element_type=F32)
            + jnp.dot(d_up[e].astype(BF16), wu[e], preferred_element_type=F32)
            for e in every
        ],
        partmsg,
    )
    send_back(partmsg, backbuf, 4)
    hidden_units = wg.shape[1]
    block = block_of(hidden_units)
    for e in every:
        dt_out[e, 0] = d_gate[e].T.astype(BF16)
        dt_out[e, 1] = d_up[e].T.astype(BF16)
        hidden_out[e] = hidden[e].T.astype(BF16)

        def grads(i, carry):
            at = pl.ds(pl.multiple_of(i * block, block), block)
            for j, out in enumerate((gate_out, up_out)):
                out[e, at, :] = jnp.dot(
                    dt_out[e, j, at, :], x_out[e], preferred_element_type=F32
                ).astype(BF16)
            return carry

        lax.fori_loop(0, hidden_units // block, grads, 0)
    bulk_wait(backbuf, n - 1, recv_sem.at[4])
    back_out[...] = backbuf[...]
    bulk_wait(xbuf.at[0], n_chip - 1, send_sem.at[0])
    bulk_wait(dybuf.at[0], n_chip - 1, send_sem.at[2])
    bulk_wait(partmsg, n - 1, send_sem.at[4])


def store_kernel(
    n_dp,
    n_ex,
    picks_hbm,
    back_in,
    gate_in,
    up_in,
    dy_in,
    hidden_in,
    tokens_out,
    gate_out,
    up_out,
    down_out,
    picks_ref,
    raw,
    wide,
    back,
    total,
    dy,
    hidden,
    down,
    sem,
    store_sem,
):
    experts, hidden_units, _ = gate_in.shape
    stores = []

    def store(src, dst):
        stores.append(pltpu.make_async_copy(src, dst, store_sem.at[len(stores)]))
        stores[-1].start()

    loads = [
        pltpu.make_async_copy(src, dst, sem.at[i])
        for i, (src, dst) in enumerate(
            ((dy_in, dy), (hidden_in, hidden), (back_in, raw), (picks_hbm, picks_ref))
        )
    ]
    for load in loads:
        load.start()
    for e in range(experts):
        store(gate_in.at[e], gate_out.at[e])
        store(up_in.at[e], up_out.at[e])
    loads[0].wait()
    loads[1].wait()
    block = block_of(hidden_units)
    for e in range(experts):

        def grads(i, carry):
            at = pl.ds(pl.multiple_of(i * block, block), block)
            down[e, at, :] = jnp.dot(
                hidden[e, at, :], dy[e], preferred_element_type=F32
            ).astype(BF16)
            return carry

        lax.fori_loop(0, hidden_units // block, grads, 0)
        store(down.at[e], down_out.at[e])
    token_rows = total.shape[0]
    loads[2].wait()
    unpack(raw, wide, back)
    loads[3].wait()
    picks = picks_ref[...].astype(F32)
    columns = lax.broadcasted_iota(jnp.int32, (picks.shape[1], n_dp * n_ex), 0)
    places = lax.broadcasted_iota(jnp.int32, (picks.shape[1], n_dp * n_ex), 1)
    summed = jnp.zeros(total.shape, F32)
    for e in range(experts):
        wanted = jnp.where(columns == lax.rem(places, n_ex) * experts + e, 1.0, 0.0)
        row = jnp.dot(
            jnp.broadcast_to(picks, (8, picks.shape[1])).astype(BF16),
            wanted.astype(BF16),
            preferred_element_type=F32,
        )[:1]
        chosen = jnp.where(
            lax.broadcasted_iota(jnp.int32, (token_rows, n_dp * n_ex), 0).astype(F32) == row,
            1.0,
            0.0,
        ).astype(BF16)
        summed += jnp.dot(chosen, back[e], preferred_element_type=F32)
    total[...] = summed.astype(BF16)
    store(total, tokens_out)
    for copy in stores:
        copy.wait()


def shards(n_dp, n_ex, tokens, cotangent, picks, gates, w_gate, w_up, w_down):
    picks, gates, tokens, cotangent, w_gate, w_up, w_down = (
        pltpu.with_memory_space_constraint(a, pltpu.HBM)
        for a in (picks, gates, tokens, cotangent, w_gate, w_up, w_down)
    )
    token_rows, width = tokens.shape
    experts, hidden, _ = w_gate.shape
    n = n_dp * n_ex
    rows = (experts, n, width)
    message = (experts * width // LANES, LANES)
    weight = pltpu.VMEM((experts, hidden, width), BF16)
    vmem = pl.BlockSpec(memory_space=pltpu.VMEM)
    anywhere = pl.BlockSpec(memory_space=pl.ANY)
    back, d_gate, d_up, dy, hid = pl.pallas_call(
        functools.partial(exchange_kernel, n_dp, n_ex),
        out_shape=(pltpu.VMEM((n,) + message, BF16),)
        + (weight,) * 2
        + (pltpu.VMEM(rows, BF16), pltpu.VMEM((experts, hidden, n), BF16)),
        in_specs=[anywhere] * 7,
        out_specs=(vmem,) * 5,
        scratch_shapes=[
            pltpu.VMEM(rows, BF16),
            pltpu.VMEM((experts, 2, hidden, n), BF16),
            pltpu.VMEM(picks.shape, jnp.int32),
            pltpu.VMEM(gates.shape, F32),
            pltpu.VMEM((token_rows, width), BF16),
            pltpu.VMEM((token_rows, width), BF16),
            weight,
            weight,
            weight,
            pltpu.VMEM((n * experts * width // LANES, LANES), F32),
            pltpu.VMEM((n_ex,) + message, BF16),
            pltpu.VMEM((n_ex,) + message, BF16),
            pltpu.VMEM((2, n // 2) + message, BF16),
            pltpu.VMEM((2, n // 2) + message, BF16),
            pltpu.VMEM((n,) + message, BF16),
            pltpu.VMEM((n,) + message, BF16),
            pltpu.SemaphoreType.DMA((7,)),
            pltpu.SemaphoreType.DMA((5,)),
            pltpu.SemaphoreType.DMA((5,)),
        ],
        compiler_params=pltpu.CompilerParams(
            collective_id=0, has_side_effects=True, vmem_limit_bytes=28 * 1024 * 1024
        ),
    )(picks, gates, tokens, cotangent, w_gate, w_up, w_down)

    grad = jax.ShapeDtypeStruct(w_gate.shape, BF16)
    return pl.pallas_call(
        functools.partial(store_kernel, n_dp, n_ex),
        out_shape=(jax.ShapeDtypeStruct(tokens.shape, BF16), grad, grad, grad),
        in_specs=[anywhere] * 6,
        out_specs=(anywhere,) * 4,
        scratch_shapes=[
            pltpu.VMEM(picks.shape, jnp.int32),
            pltpu.VMEM((n,) + message, BF16),
            pltpu.VMEM((n * experts * width // LANES, LANES), F32),
            pltpu.VMEM(rows, BF16),
            pltpu.VMEM(tokens.shape, BF16),
            pltpu.VMEM(rows, BF16),
            pltpu.VMEM((experts, hidden, n), BF16),
            weight,
            pltpu.SemaphoreType.DMA((4,)),
            pltpu.SemaphoreType.DMA((3 * experts + 1,)),
        ],
        compiler_params=pltpu.CompilerParams(vmem_limit_bytes=16 * 1024 * 1024),
    )(picks, back, d_gate, d_up, dy, hid)


def solution(mesh):
    spread = P(("dp", "expert"), None)
    weight = P("expert", "dp", None)
    return jax.shard_map(
        functools.partial(shards, mesh.shape["dp"], mesh.shape["expert"]),
        mesh=mesh,
        in_specs=(spread,) * 4 + (weight,) * 3,
        out_specs=(spread,) + (weight,) * 3,
        check_vma=False,
    )
```

```python
import functools

import jax
import jax.numpy as jnp
from jax import lax
from jax.experimental import pallas as pl
from jax.experimental.pallas import tpu as pltpu
from jax.sharding import PartitionSpec as P

LANES = 128
BF16 = jnp.bfloat16
F32 = jnp.float32
NT = (((1,), (1,)), ((), ()))


def block_of(hidden_units):
    return max(d for d in range(16, 177, 16) if hidden_units % d == 0)


def bulk_wait(ref, count, sem):
    part = ref.at[pl.ds(0, count)]
    pltpu.make_async_copy(part, part, sem).wait()


def unpack(buf, wide, out):
    experts, n, width = out.shape
    chunks = width // LANES
    wide[...] = buf[...].reshape(wide.shape).astype(F32)
    for e in range(experts):
        for k in range(chunks):
            out[e, :, k * LANES : (k + 1) * LANES] = wide[
                pl.ds(e * chunks + k, n, stride=experts * chunks), :
            ].astype(BF16)


def exchange_kernel(
    n_dp,
    n_ex,
    picks_hbm,
    gates_hbm,
    tokens_hbm,
    cot_hbm,
    wg_hbm,
    wu_hbm,
    wd_hbm,
    back_out,
    gate_out,
    up_out,
    down_out,
    x_out,
    dy_out,
    dt_out,
    picks_ref,
    gates_ref,
    tok,
    cot,
    wg,
    wu,
    wd,
    wide,
    xmsg,
    dymsg,
    xbuf,
    dybuf,
    partmsg,
    pairbuf,
    summsg,
    backbuf,
    load_sem,
    send_sem,
    recv_sem,
):
    n = n_dp * n_ex
    experts, _, width = wg.shape
    chunks = width // LANES
    picked = picks_ref.shape[1]
    token_rows = tok.shape[0]
    my_dp, my_ex = lax.axis_index("dp"), lax.axis_index("expert")
    cores = 2
    n_chip = n // cores
    my_core, my_half = lax.rem(my_dp, cores), my_dp // cores
    my_chip = my_half * n_ex + my_ex

    loads = [
        pltpu.make_async_copy(src, dst, load_sem.at[i])
        for i, (src, dst) in enumerate(
            (
                (picks_hbm, picks_ref),
                (tokens_hbm, tok),
                (gates_hbm, gates_ref),
                (cot_hbm, cot),
                (wg_hbm, wg),
                (wu_hbm, wu),
                (wd_hbm, wd),
            )
        )
    ]
    for load in loads:
        load.start()

    def wrap(value, size):
        return jnp.where(value >= size, value - size, value)

    experts_at = [wrap(my_ex + b, n_ex) for b in range(n_ex)]

    def each_chip(act):
        for b in range(1, n_ex):
            act(my_half, experts_at[b])

        def ring(a, carry):
            half = wrap(my_half + a, n_dp // cores)
            for b in range(n_ex):
                act(half, experts_at[b])
            return carry

        lax.fori_loop(1, n_dp // cores, ring, 0)

    sibling = (my_half * cores + 1 - my_core, my_ex)

    barrier = pltpu.get_barrier_semaphore()

    def greet(where):
        pl.semaphore_signal(
            barrier, inc=1, device_id=where, device_id_type=pl.DeviceIdType.MESH
        )

    def greet_chip(half, ex):
        greet((half * cores + my_core, ex))

    greet(sibling)
    each_chip(greet_chip)

    eye = lax.broadcasted_iota(jnp.int32, (picked, picked), 0) == lax.broadcasted_iota(
        jnp.int32, (picked, picked), 1
    )
    loads[0].wait()
    pick_col = jnp.sum(
        jnp.where(eye, picks_ref[...].astype(F32), 0.0), axis=1, keepdims=True
    ).astype(jnp.int32)
    selector = jnp.where(
        lax.broadcasted_iota(jnp.int32, (picked, token_rows), 1) == pick_col, 1.0, 0.0
    ).astype(BF16)

    def pack(parts, msg):
        count = parts[0].shape[0]
        stride = len(parts) * chunks
        for e, value in enumerate(parts):
            for k in range(chunks):
                wide[pl.ds(e * chunks + k, count, stride=stride), :] = value[
                    :, k * LANES : (k + 1) * LANES
                ]
        msg[...] = wide[pl.ds(0, count * stride), :].astype(BF16).reshape(msg.shape)

    def remote(src, dst, slot, where):
        return pltpu.make_async_remote_copy(
            src_ref=src,
            dst_ref=dst,
            send_sem=send_sem.at[slot],
            recv_sem=recv_sem.at[slot],
            device_id=where,
            device_id_type=pl.DeviceIdType.MESH,
        )

    def send_chips(msg, buf, slot):
        def one(half, ex):
            where = (half * cores + my_core, ex)
            remote(msg.at[ex], buf.at[my_core, my_chip], slot, where).start()

        each_chip(one)
        buf[my_core, my_chip] = msg[my_ex]

    def hand_over(buf, slot):
        bulk_wait(buf.at[0], n_chip - 1, recv_sem.at[slot])
        copy = remote(buf.at[my_core], buf.at[my_core], slot + 1, sibling)
        copy.start()
        return copy

    loads[1].wait()
    pack([jnp.dot(selector, tok[...], preferred_element_type=F32)], xmsg)
    pl.semaphore_wait(barrier, n_chip)
    send_chips(xmsg, xbuf, 0)
    loads[2].wait()
    gate_col = jnp.sum(jnp.where(eye, gates_ref[...], 0.0), axis=1, keepdims=True)
    loads[3].wait()
    pack([jnp.dot(selector, cot[...], preferred_element_type=F32) * gate_col], dymsg)
    send_chips(dymsg, dybuf, 2)

    def forward(e, value, weights):
        return lax.dot_general(value[e], weights[e], NT, preferred_element_type=F32)

    every = range(experts)
    x_copy = hand_over(xbuf, 0)
    x_copy.wait()
    unpack(xbuf, wide, x_out)
    loads[4].wait()
    pre_gate = [forward(e, x_out, wg) for e in every]
    loads[5].wait()
    dy_copy = hand_over(dybuf, 2)
    pre_up = [forward(e, x_out, wu) for e in every]
    sigmoid_g = [jax.nn.sigmoid(g) for g in pre_gate]
    active = [g * s for g, s in zip(pre_gate, sigmoid_g)]
    slope = [
        u * s * (1.0 + g * (1.0 - s)) for g, u, s in zip(pre_gate, pre_up, sigmoid_g)
    ]
    hidden = [a * u for a, u in zip(active, pre_up)]
    loads[6].wait()
    dy_copy.wait()
    unpack(dybuf, wide, dy_out)
    grad_hidden = [forward(e, dy_out, wd) for e in every]
    d_up = [h * a for h, a in zip(grad_hidden, active)]
    d_gate = [h * s for h, s in zip(grad_hidden, slope)]
    pack(
        [
            jnp.dot(d_gate[e].astype(BF16), wg[e], preferred_element_type=F32)
            + jnp.dot(d_up[e].astype(BF16), wu[e], preferred_element_type=F32)
            for e in every
        ],
        partmsg,
    )
    pair = remote(partmsg.at[1 - my_core], pairbuf, 4, sibling)
    pair.start()
    hidden_units = wg.shape[1]
    block = block_of(hidden_units)
    for e in every:
        dt_out[e, 0] = d_gate[e].T.astype(BF16)
        dt_out[e, 1] = d_up[e].T.astype(BF16)
        dt_out[e, 2] = hidden[e].T.astype(BF16)
    pair.wait()
    own_rows = n_chip * experts * chunks
    own = wide[pl.ds(pl.multiple_of(my_core * own_rows, own_rows), own_rows), :]
    summed = own + pairbuf[...].reshape(own.shape).astype(F32)
    summsg[...] = summed.astype(BF16).reshape(summsg.shape)

    def send_back(half, ex):
        where = (half * cores + my_core, ex)
        remote(summsg.at[half * n_ex + ex], backbuf.at[my_chip], 5, where).start()

    each_chip(send_back)
    backbuf[my_chip] = summsg[my_chip]
    for e in every:

        def grads(i, carry):
            at = pl.ds(pl.multiple_of(i * block, block), block)
            for j, (out, other) in enumerate(
                ((gate_out, x_out), (up_out, x_out), (down_out, dy_out))
            ):
                out[e, at, :] = jnp.dot(
                    dt_out[e, j, at, :], other[e], preferred_element_type=F32
                ).astype(BF16)
            return carry

        lax.fori_loop(0, hidden_units // block, grads, 0)
    bulk_wait(backbuf, n_chip - 1, recv_sem.at[5])
    back_out[...] = backbuf[...]
    bulk_wait(xbuf.at[0], n_chip - 1, send_sem.at[0])
    bulk_wait(dybuf.at[0], n_chip - 1, send_sem.at[2])
    bulk_wait(summsg, n_chip - 1, send_sem.at[5])


def store_kernel(
    n_ex,
    picks_hbm,
    back_in,
    gate_in,
    up_in,
    down_in,
    tokens_out,
    gate_out,
    up_out,
    down_out,
    picks_ref,
    raw,
    wide,
    back,
    total,
    sem,
    store_sem,
):
    picks_load = pltpu.make_async_copy(picks_hbm, picks_ref, sem.at[0])
    picks_load.start()
    load = pltpu.make_async_copy(back_in, raw, sem.at[2])
    load.start()
    experts, hidden_units, _ = gate_in.shape
    half = hidden_units // 2 // 16 * 16
    stores = []
    for e in range(experts):
        for src, dst in ((gate_in, gate_out), (up_in, up_out), (down_in, down_out)):
            for at in (pl.ds(0, half), pl.ds(half, hidden_units - half)):
                stores.append(
                    pltpu.make_async_copy(
                        src.at[e, at], dst.at[e, at], store_sem.at[len(stores)]
                    )
                )
                stores[-1].start()
    token_rows, sources = total.shape[0], back.shape[1]
    load.wait()
    unpack(raw, wide, back)
    picks_load.wait()
    picks = picks_ref[...].astype(F32)
    columns = lax.broadcasted_iota(jnp.int32, (picks.shape[1], sources), 0)
    places = lax.broadcasted_iota(jnp.int32, (picks.shape[1], sources), 1)
    summed = jnp.zeros(total.shape, F32)
    for e in range(experts):
        wanted = jnp.where(columns == lax.rem(places, n_ex) * experts + e, 1.0, 0.0)
        row = jnp.dot(
            jnp.broadcast_to(picks, (8, picks.shape[1])).astype(BF16),
            wanted.astype(BF16),
            preferred_element_type=F32,
        )[:1]
        chosen = jnp.where(
            lax.broadcasted_iota(jnp.int32, (token_rows, sources), 0).astype(F32) == row,
            1.0,
            0.0,
        ).astype(BF16)
        summed += jnp.dot(chosen, back[e], preferred_element_type=F32)
    total[...] = summed.astype(BF16)
    stores.append(pltpu.make_async_copy(total, tokens_out, sem.at[1]))
    stores[-1].start()
    for store in stores:
        store.wait()


def shards(n_dp, n_ex, tokens, cotangent, picks, gates, w_gate, w_up, w_down):
    picks, gates, tokens, cotangent, w_gate, w_up, w_down = (
        pltpu.with_memory_space_constraint(a, pltpu.HBM)
        for a in (picks, gates, tokens, cotangent, w_gate, w_up, w_down)
    )
    token_rows, width = tokens.shape
    experts, hidden, _ = w_gate.shape
    n = n_dp * n_ex
    rows = (experts, n, width)
    message = (experts * width // LANES, LANES)
    weight = pltpu.VMEM((experts, hidden, width), BF16)
    vmem = pl.BlockSpec(memory_space=pltpu.VMEM)
    anywhere = pl.BlockSpec(memory_space=pl.ANY)
    back, d_gate, d_up, d_down = pl.pallas_call(
        functools.partial(exchange_kernel, n_dp, n_ex),
        out_shape=(pltpu.VMEM((n // 2,) + message, BF16),) + (weight,) * 3,
        in_specs=[anywhere] * 7,
        out_specs=(vmem,) * 4,
        scratch_shapes=[
            pltpu.VMEM(rows, BF16),
            pltpu.VMEM(rows, BF16),
            pltpu.VMEM((experts, 3, hidden, n), BF16),
            pltpu.VMEM(picks.shape, jnp.int32),
            pltpu.VMEM(gates.shape, F32),
            pltpu.VMEM((token_rows, width), BF16),
            pltpu.VMEM((token_rows, width), BF16),
            weight,
            weight,
            weight,
            pltpu.VMEM((n * experts * width // LANES, LANES), F32),
            pltpu.VMEM((n_ex,) + message, BF16),
            pltpu.VMEM((n_ex,) + message, BF16),
            pltpu.VMEM((2, n // 2) + message, BF16),
            pltpu.VMEM((2, n // 2) + message, BF16),
            pltpu.VMEM((2, n // 2) + message, BF16),
            pltpu.VMEM((n // 2,) + message, BF16),
            pltpu.VMEM((n // 2,) + message, BF16),
            pltpu.VMEM((n // 2,) + message, BF16),
            pltpu.SemaphoreType.DMA((7,)),
            pltpu.SemaphoreType.DMA((6,)),
            pltpu.SemaphoreType.DMA((6,)),
        ],
        compiler_params=pltpu.CompilerParams(
            collective_id=0, has_side_effects=True, vmem_limit_bytes=28 * 1024 * 1024
        ),
    )(picks, gates, tokens, cotangent, w_gate, w_up, w_down)

    grad = jax.ShapeDtypeStruct(w_gate.shape, BF16)
    return pl.pallas_call(
        functools.partial(store_kernel, n_ex),
        out_shape=(jax.ShapeDtypeStruct(tokens.shape, BF16), grad, grad, grad),
        in_specs=[anywhere] * 5,
        out_specs=(anywhere,) * 4,
        scratch_shapes=[
            pltpu.VMEM(picks.shape, jnp.int32),
            pltpu.VMEM((n // 2,) + message, BF16),
            pltpu.VMEM((n * experts * width // LANES // 2, LANES), F32),
            pltpu.VMEM((experts, n // 2, width), BF16),
            pltpu.VMEM(tokens.shape, BF16),
            pltpu.SemaphoreType.DMA((3,)),
            pltpu.SemaphoreType.DMA((6 * experts,)),
        ],
        compiler_params=pltpu.CompilerParams(vmem_limit_bytes=16 * 1024 * 1024),
    )(picks, back, d_gate, d_up, d_down)


def solution(mesh):
    spread = P(("dp", "expert"), None)
    weight = P("expert", "dp", None)
    return jax.shard_map(
        functools.partial(shards, mesh.shape["dp"], mesh.shape["expert"]),
        mesh=mesh,
        in_specs=(spread,) * 4 + (weight,) * 3,
        out_specs=(spread,) + (weight,) * 3,
        check_vma=False,
    )
```
